512 devices in a mesh: outer: 16 (over x, y), inner: 32 (over z, core).
Axes of the slice: x: 4, y: 4, z: 16, core: 2. Of those that a mesh axis runs over, the one named last changes fastest.
Arguments:
- x_raw: bfloat16 [2, 4096, 4096], P(None, 'inner', 'outer'), may hold values from -6 to 6
- bc_raw: bfloat16 [2, 4096, 512], P(None, 'inner'), may hold values from -6 to 6
- step_raw: float32 [2, 4096, 64], P(None, 'inner', 'outer'), may hold values from -3 to 3
- lengths: int32 [2], replicated, may hold values from 2048 to 4096, as said below
- conv_weight_x: float32 [4, 4096], P(None, 'outer'), may hold values from -3 to 3
- conv_bias_x: float32 [4096], P('outer'), may hold values from -3 to 3
- conv_weight_bc: float32 [4, 512], replicated, may hold values from -3 to 3
- conv_bias_bc: float32 [512], replicated, may hold values from -3 to 3
- step_bias: float32 [64], P('outer'), may hold values from -4 to -3
- decay_log: float32 [64], P('outer')
- skip_gain: float32 [64], P('outer'), may hold values from 0.5 to 1.5
- output_grad: bfloat16 [2, 4096, 4096], P(None, 'inner', 'outer'), may hold values from -6 to 6
Outputs:
- mixer_out: bfloat16 [2, 4096, 4096], P(None, 'inner', 'outer')
- grad_x: bfloat16 [2, 4096, 4096], P(None, 'inner', 'outer')
- grad_bc: bfloat16 [2, 4096, 512], P(None, 'inner')
- grad_step_raw: float32 [2, 4096, 64], P(None, 'inner', 'outer')
- grad_conv_weight_x: float32 [4, 4096], P(None, 'outer')
- grad_conv_bias_x: float32 [4096], P('outer')
- grad_conv_weight_bc: float32 [4, 512], replicated
- grad_conv_bias_bc: float32 [512], replicated
- grad_step_bias: float32 [64], P('outer')
- grad_decay_log: float32 [64], P('outer')
- grad_skip_gain: float32 [64], P('outer')
The draws below stay inside these ranges and needn't reach their ends.
Inputs may be any that keep to these rules, and one draw needn't show every extreme that they name: One of the two lengths is 4096; the other is at least 2048.
All inputs are finite; a program needn't handle non-finite values.
Results may differ from the reference program's by a relative error of at most 0.001.
Values may be sent and summed in bfloat16 or wider, within the bound.
A program may use at most 64 MiB of HBM per device.

```python
import math
import jax
import jax.numpy as jnp
from jax import lax

H = 64
P_SIZE = 64
N = 256
KW = 4
XBC = 4608
SEQ = 4096


def draw_lengths(key, part):
    key = jax.random.fold_in(key, 11)
    first_key, second_key = jax.random.split(key)
    which_full = jax.random.randint(first_key, (), 0, 2)
    other_len = jax.random.randint(second_key, (), SEQ // 2, SEQ + 1)
    return jnp.where(jnp.arange(2) == which_full, SEQ, other_len).astype(jnp.int32)


def draw_decay_log(key, part):
    key = jax.random.fold_in(key, 5)
    order_key, fast_key, slow_key = jax.random.split(key, 3)
    order = jax.random.permutation(order_key, H)
    quick_count = H // 2
    fast_heads = order < quick_count
    rapid = jax.random.uniform(fast_key, (H,), jnp.float32, 0.4, 1.6)
    gentle = jnp.exp(jax.random.uniform(slow_key, (H,), jnp.float32, math.log(5.0), math.log(50.0))) / SEQ
    return jnp.log(jnp.where(fast_heads, rapid, gentle)).astype(jnp.float32)


def levels(own_key, shape, cuts, smallest, top_value):
    loudness = 1.0
    for dim, parts in cuts:
        draws = jax.random.uniform(jax.random.fold_in(jax.random.fold_in(own_key, 6), dim), (parts,), jnp.float32, smallest / len(cuts), top_value / len(cuts))
        loudness = loudness * jnp.repeat(jnp.exp(draws), shape[dim] // parts).reshape((-1,) + (1,) * (len(shape) - 1 - dim))
    return loudness


def scatter_about(rng, dims, width, reach, shards=(), kind=jnp.bfloat16):
    drawn = jax.random.normal(rng, dims, jnp.float32) * width
    if len(shards) > 0:
        drawn = levels(rng, dims, shards, -0.22, 0.18) * drawn
    return jnp.clip(drawn, min=-reach, max=reach).astype(kind)


def setup_inputs(seed: int = 0) -> dict:
    keys = jax.random.split(jax.random.key(seed), 13)
    x_raw = scatter_about(keys[0], (2, SEQ, H * P_SIZE), 1.0, 6.0, ((1, 32), (2, 16)))
    bc_raw = scatter_about(keys[1], (2, SEQ, 2 * N), 1.0, 6.0, ((1, 32),))
    step_raw = scatter_about(keys[2], (2, SEQ, H), 0.5, 3.0, ((1, 32), (2, 16)), jnp.float32)
    lengths = draw_lengths(jax.random.fold_in(keys[12], 71), 0)
    conv_weight_x = scatter_about(keys[4], (KW, H * P_SIZE), KW ** -0.5, 3.0, ((1, 16),), jnp.float32)
    conv_bias_x = scatter_about(keys[5], (H * P_SIZE,), 0.5, 3.0, ((0, 16),), jnp.float32)
    conv_weight_bc = scatter_about(keys[6], (KW, 2 * N), KW ** -0.5, 3.0, (), jnp.float32)
    conv_bias_bc = scatter_about(keys[7], (2 * N,), 0.5, 3.0, (), jnp.float32)
    step_bias = jnp.clip(-4.0 + 1.0 * jax.random.uniform(keys[8], (H,), jnp.float32) ** levels(keys[8], (H,), ((0, 16),), -0.2, 0.2), -4.0, -3.0)
    decay_log = draw_decay_log(jax.random.fold_in(keys[12], 71), 0)
    skip_gain = jnp.clip(0.5 + 1.0 * jax.random.uniform(keys[10], (H,), jnp.float32) ** levels(keys[10], (H,), ((0, 16),), -0.2, 0.2), 0.5, 1.5)
    output_grad = scatter_about(keys[11], (2, SEQ, H * P_SIZE), 1.0, 6.0, ((1, 32), (2, 16)))
    return {"x_raw": x_raw, "bc_raw": bc_raw, "step_raw": step_raw, "lengths": lengths, "conv_weight_x": conv_weight_x, "conv_bias_x": conv_bias_x, "conv_weight_bc": conv_weight_bc, "conv_bias_bc": conv_bias_bc, "step_bias": step_bias, "decay_log": decay_log, "skip_gain": skip_gain, "output_grad": output_grad}


HIGH = lax.Precision.HIGHEST

def seq_forward(raw_float, step_raw, seq_length, conv_weight, conv_bias, step_bias, decay_log, skip_gain):
    padded = jnp.concatenate([jnp.zeros((KW - 1, XBC), jnp.float32), raw_float], axis=0)
    pre_act = conv_bias
    for offset in range(KW):
        pre_act = pre_act + conv_weight[offset] * padded[offset:offset + SEQ]
    activated = jax.nn.silu(pre_act)
    features = activated[:, :H * P_SIZE].reshape(SEQ, H, P_SIZE)
    key_rows = activated[:, H * P_SIZE:H * P_SIZE + N]
    query_rows = activated[:, H * P_SIZE + N:]
    position = jnp.arange(SEQ, dtype=jnp.int32)
    valid_mask = (position < seq_length).astype(jnp.float32)
    step_size = jax.nn.softplus(step_raw + step_bias) * valid_mask[:, None]
    log_decay = step_size * -jnp.exp(decay_log)
    block_len = math.gcd(SEQ, 128)
    block_count = SEQ // block_len
    causal = jnp.arange(block_len)[:, None] >= jnp.arange(block_len)[None, :]

    def one_block(state_carry, pieces):
        feat_b, key_b, query_b, step_b, logs_b = pieces
        cumulative = jnp.cumsum(logs_b, axis=0)
        scores = jnp.dot(query_b, key_b.T, precision=HIGH)
        log_gap = cumulative[:, None, :] - cumulative[None, :, :]
        decays = jnp.where(causal[:, :, None], jnp.exp(jnp.where(causal[:, :, None], log_gap, 0.0)), 0.0)
        mixing = decays * scores[:, :, None] * step_b[None, :, :]
        within = jnp.einsum('tuh,uhp->thp', mixing, feat_b, precision=HIGH)
        carried = jnp.einsum('tn,hpn->thp', query_b, state_carry, precision=HIGH) * jnp.exp(cumulative)[:, :, None]
        block_total = cumulative[-1]
        weight = jnp.exp(block_total[None, :] - cumulative) * step_b
        local_state = jnp.einsum('uh,uhp,un->hpn', weight, feat_b, key_b, precision=HIGH)
        new_state = jnp.exp(block_total)[:, None, None] * state_carry + local_state
        return (new_state, within + carried)
    pieces = (features.reshape(block_count, block_len, H, P_SIZE), key_rows.reshape(block_count, block_len, N), query_rows.reshape(block_count, block_len, N), step_size.reshape(block_count, block_len, H), log_decay.reshape(block_count, block_len, H))
    _, outputs = lax.scan(one_block, jnp.zeros((H, P_SIZE, N), jnp.float32), pieces)
    mixed = outputs.reshape(SEQ, H, P_SIZE) + skip_gain[None, :, None] * features
    return (mixed * valid_mask[:, None, None]).reshape(SEQ, H * P_SIZE)

def reference(x_raw, bc_raw, step_raw, lengths, conv_weight_x, conv_bias_x, conv_weight_bc, conv_bias_bc, step_bias, decay_log, skip_gain, output_grad):

    def both(raw_float, steps_all, weight, bias, sbias, dlog, skip):
        outs = [seq_forward(raw_float[which_seq], steps_all[which_seq], lengths[which_seq], weight, bias, sbias, dlog, skip) for which_seq in range(2)]
        return jnp.stack(outs, axis=0)
    raw_float = jnp.concatenate([x_raw, bc_raw], axis=2).astype(jnp.float32)
    conv_weight = jnp.concatenate([conv_weight_x, conv_weight_bc], axis=1)
    conv_bias = jnp.concatenate([conv_bias_x, conv_bias_bc], axis=0)
    result, back_fn = jax.vjp(both, raw_float, step_raw, conv_weight, conv_bias, step_bias, decay_log, skip_gain)
    grads = back_fn(output_grad.astype(jnp.float32))
    split_at = H * P_SIZE
    return (result.astype(jnp.bfloat16), grads[0][..., :split_at].astype(jnp.bfloat16), grads[0][..., split_at:].astype(jnp.bfloat16), grads[1], grads[2][:, :split_at], grads[3][:split_at], grads[2][:, split_at:], grads[3][split_at:], grads[4], grads[5], grads[6])
```

```python
import functools

import jax
import jax.numpy as jnp
from jax import lax
from jax.experimental import pallas as pl
from jax.experimental.pallas import tpu as pltpu
from jax.sharding import PartitionSpec as P

P_SIZE = 64
F32 = jnp.float32
BF = jnp.bfloat16
MESH = pl.DeviceIdType.MESH
VMEM = pltpu.VMEM
DMA = pltpu.SemaphoreType.DMA
LIMIT = 48 * 1024 * 1024
NN = ((1,), (0,))
NT = ((1,), (1,))
TN = ((0,), (0,))


def dot(a, b, dims):
    return lax.dot_general(a, b, (dims, ((), ())), preferred_element_type=F32)


def split(a):
    high = a.astype(BF)
    return high, (a - high.astype(F32)).astype(BF)


def split3(a):
    high = a.astype(BF)
    rest = a - high.astype(F32)
    mid = rest.astype(BF)
    return high, mid, (rest - mid.astype(F32)).astype(BF)


def mm(a, b, dims):
    out = dot(a[0], b[0], dims)
    if len(b) > 1:
        out = out + dot(a[0], b[1], dims)
    if len(a) > 1:
        out = out + dot(a[1], b[0], dims)
    return out


def mm_exact(parts, ones, dims):
    out = dot(parts[0], ones, dims)
    for part in parts[1:]:
        out = out + dot(part, ones, dims)
    return out


def mm_exact_left(ones, parts, dims):
    out = dot(ones, parts[0], dims)
    for part in parts[1:]:
        out = out + dot(ones, part, dims)
    return out


def iota(shape, dim):
    return lax.broadcasted_iota(jnp.int32, shape, dim)


def spread(per_head, width):
    rows, heads = per_head.shape
    lane = iota((rows, width), 1)
    out = jnp.broadcast_to(per_head[:, 0:1], (rows, width))
    for head in range(1, heads):
        out = jnp.where(lane >= head * P_SIZE, per_head[:, head : head + 1], out)
    return out


def head_ones(width, heads):
    row, col = iota((width, heads), 0), iota((width, heads), 1)
    return jnp.where((row >= col * P_SIZE) & (row < (col + 1) * P_SIZE), 1.0, 0.0).astype(BF)


def triangle(rows, upper):
    row, col = iota((rows, rows), 0), iota((rows, rows), 1)
    return jnp.where(col >= row if upper else row >= col, 1.0, 0.0).astype(BF)


def convolved(ext_ref, start, weight, bias, row_count):
    pre_act = bias
    for tap in range(weight.shape[0]):
        pre_act = pre_act + weight[tap : tap + 1] * ext_ref[start + tap : start + tap + row_count, :]
    return pre_act


def softplus(z):
    return jnp.maximum(z, 0.0) + jnp.log1p(jnp.exp(-jnp.abs(z)))


def sigmoid(z):
    return 1.0 / (1.0 + jnp.exp(-z))


def valid_rows(lengths_ref, seq, row_count):
    first = lax.axis_index("inner") * row_count
    return jnp.where(first + iota((row_count, 1), 0) < lengths_ref[seq], 1.0, 0.0)


def edges_kernel(size, x_ref, bc_ref, px_ref, pbc_ref, nbc_ref, send_sem, recv_sem):
    me = lax.axis_index("inner")
    after, before = lax.rem(me + 1, size), lax.rem(me + size - 1, size)
    row_count, edge = x_ref.shape[1], px_ref.shape[1]
    barrier = pltpu.get_barrier_semaphore()
    for other in (after, before):
        pl.semaphore_signal(barrier, inc=1, device_id={"inner": other}, device_id_type=MESH)
    pl.semaphore_wait(barrier, 2)
    last = pl.ds(row_count - edge, edge)
    copies = []
    for i, (src, dst, other) in enumerate(
        (
            (x_ref.at[:, last, :], px_ref, after),
            (bc_ref.at[:, last, :], pbc_ref, after),
            (bc_ref.at[:, pl.ds(0, edge), :], nbc_ref, before),
        )
    ):
        copies.append(
            pltpu.make_async_remote_copy(
                src_ref=src, dst_ref=dst, send_sem=send_sem.at[i], recv_sem=recv_sem.at[i],
                device_id={"inner": other}, device_id_type=MESH,
            )
        )
        copies[-1].start()
    for copy in copies:
        copy.wait()


def edges(x_raw, bc_raw, size, edge):
    seqs, _, wide = x_raw.shape
    both = bc_raw.shape[2]
    return pl.pallas_call(
        functools.partial(edges_kernel, size),
        out_shape=[
            jax.ShapeDtypeStruct((seqs, edge, wide), BF),
            jax.ShapeDtypeStruct((seqs, edge, both), BF),
            jax.ShapeDtypeStruct((seqs, edge, both), BF),
        ],
        in_specs=[pl.BlockSpec(memory_space=VMEM)] * 2,
        out_specs=[pl.BlockSpec(memory_space=VMEM)] * 3,
        scratch_shapes=[DMA((3,)), DMA((3,))],
        compiler_params=pltpu.CompilerParams(collective_id=0, has_side_effects=True),
    )(x_raw, bc_raw)


def front_kernel(
    lengths_ref, x_ref, bc_ref, px_ref, pbc_ref, step_ref, og_ref, wx_ref, bx_ref, wbc_ref, bbc_ref, sb_ref, dl_ref,
    states_ref, decay_ref, feat_ref, slope_ref, kq_ref, dt_ref, cum_ref, extx_ref, extbc_ref,
):
    seq = pl.program_id(0)
    row_count, wide = x_ref.shape[1:]
    edge, taps = px_ref.shape[1], wx_ref.shape[0]
    heads, state = step_ref.shape[2], wbc_ref.shape[1] // 2
    keep = jnp.where(lax.axis_index("inner") > 0, 1.0, 0.0)
    extx_ref[:edge, :] = px_ref[0].astype(F32) * keep
    extx_ref[edge:, :] = x_ref[0].astype(F32)
    extbc_ref[:edge, :] = pbc_ref[0].astype(F32) * keep
    extbc_ref[edge:, :] = bc_ref[0].astype(F32)
    start = edge - (taps - 1)
    pre_x = convolved(extx_ref, start, wx_ref[...], bx_ref[...], row_count)
    gate = sigmoid(pre_x)
    feat = pre_x * gate
    feat_ref[0] = feat
    slope_ref[0] = gate * (1.0 + pre_x * (1.0 - gate))
    pre_bc = convolved(extbc_ref, start, wbc_ref[...], bbc_ref[...], row_count)
    kq = pre_bc * sigmoid(pre_bc)
    kq_ref[0] = kq
    valid = valid_rows(lengths_ref, seq, row_count)
    dt = softplus(step_ref[0] + sb_ref[...]) * valid
    logs = dt * -jnp.exp(dl_ref[...])
    cum = mm_exact_left(triangle(row_count, False), split3(logs), NN)
    dt_ref[0] = dt
    cum_ref[0] = cum
    total = cum[row_count - 1 : row_count, :]
    weight = spread(jnp.exp(total - cum) * dt, wide)
    grown = spread(jnp.exp(cum), wide)
    dy = og_ref[0].astype(F32) * valid
    keys, queries = split(kq[:, :state]), split(kq[:, state:])
    states_ref[0, 0] = mm(split(weight * feat), keys, TN)
    states_ref[1, 0] = mm(split(grown * dy), queries, TN)
    for head in range(heads):
        decay_ref[0, head : head + 1, :] = jnp.broadcast_to(jnp.exp(total[:, head : head + 1]), (1, state))


def front(lengths, x_raw, bc_raw, px, pbc, step_raw, output_grad, wx, bx, wbc, bbc, sb, dl):
    seqs, row_count, wide = x_raw.shape
    both, heads, edge = bc_raw.shape[2], step_raw.shape[2], px.shape[1]
    state = both // 2

    def seq_block(*shape):
        return pl.BlockSpec((1,) + shape, lambda s: (s, 0, 0))

    def whole(a):
        return pl.BlockSpec(a.shape, lambda s: (0, 0))

    return pl.pallas_call(
        front_kernel,
        grid=(seqs,),
        out_shape=[
            jax.ShapeDtypeStruct((2, seqs, wide, state), F32),
            jax.ShapeDtypeStruct((seqs, heads, state), F32),
            jax.ShapeDtypeStruct((seqs, row_count, wide), F32),
            jax.ShapeDtypeStruct((seqs, row_count, wide), F32),
            jax.ShapeDtypeStruct((seqs, row_count, both), F32),
            jax.ShapeDtypeStruct((seqs, row_count, heads), F32),
            jax.ShapeDtypeStruct((seqs, row_count, heads), F32),
        ],
        in_specs=[
            pl.BlockSpec(memory_space=pltpu.SMEM),
            seq_block(row_count, wide), seq_block(row_count, both), seq_block(edge, wide), seq_block(edge, both),
            seq_block(row_count, heads), seq_block(row_count, wide),
            whole(wx), whole(bx), whole(wbc), whole(bbc), whole(sb), whole(dl),
        ],
        out_specs=[
            pl.BlockSpec((2, 1, wide, state), lambda s: (0, s, 0, 0)),
            seq_block(heads, state), seq_block(row_count, wide), seq_block(row_count, wide), seq_block(row_count, both),
            seq_block(row_count, heads), seq_block(row_count, heads),
        ],
        scratch_shapes=[VMEM((edge + row_count, wide), F32), VMEM((edge + row_count, both), F32)],
        compiler_params=pltpu.CompilerParams(vmem_limit_bytes=LIMIT),
    )(lengths, x_raw, bc_raw, px, pbc, step_raw, output_grad, wx, bx, wbc, bbc, sb, dl)


def chain_kernel(chips, pieces, own_ref, decay_ref, out_ref, other_ref, odecay_ref, far_ref, near_ref,
                 psend, precv, dsend, drecv, fsend, frecv, nsend, nrecv):
    me = lax.axis_index("inner")
    chip, core = me // 2, lax.rem(me, 2)
    mate = chip * 2 + 1 - core
    ahead = lax.rem(chip + 1 - 2 * core + chips, chips)
    behind = lax.rem(chip - 1 + 2 * core + chips, chips)
    place = jnp.where(core == 0, chip, chips - 1 - chip)
    first, last = place == 0, place == chips - 1
    ahead, behind = ahead * 2 + core, behind * 2 + core
    seqs, heads, state = decay_ref.shape
    total_rows = own_ref.shape[1]
    rows = total_rows // pieces
    per_head = P_SIZE // rows

    barrier = pltpu.get_barrier_semaphore()
    for other in (mate, ahead, behind):
        pl.semaphore_signal(barrier, inc=1, device_id={"inner": other}, device_id_type=MESH)
    pl.semaphore_wait(barrier, 3)

    def remote(src, dst, send, recv, other):
        return pltpu.make_async_remote_copy(
            src_ref=src, dst_ref=dst, send_sem=send, recv_sem=recv, device_id={"inner": other}, device_id_type=MESH
        )

    decays = remote(decay_ref, odecay_ref, dsend.at[0], drecv.at[0], mate)
    decays.start()

    def piece(j):
        return pl.ds(pl.multiple_of(j * rows, rows), rows)

    def swap(j):
        return remote(own_ref.at[1 - core, piece(j), :], other_ref.at[piece(j), :], psend.at[j], precv.at[j], mate)

    def pass_on(j):
        return remote(far_ref.at[piece(j), :], out_ref.at[core, piece(j), :], fsend.at[j], frecv.at[j], ahead)

    def hand_over(j, slot):
        return remote(near_ref.at[piece(j), :], out_ref.at[slot, piece(j), :], nsend.at[j], nrecv.at[j], mate)

    def begin(j, carry):
        swap(j).start()
        return carry

    lax.fori_loop(0, pieces, begin, 0)
    decays.wait()

    def step(j, carry):
        @pl.when(jnp.logical_not(first))
        def _():
            pass_on(j).wait_recv()

        @pl.when(first)
        def _():
            out_ref[core, piece(j), :] = jnp.zeros((rows, state), F32)

        head = j // per_head
        seq, head = head // heads, lax.rem(head, heads)
        near = decay_ref[seq, pl.ds(head, 1), :] * out_ref[core, piece(j), :] + own_ref[core, piece(j), :]
        near_ref[piece(j), :] = near
        swap(j).wait_recv()
        far_ref[piece(j), :] = odecay_ref[seq, pl.ds(head, 1), :] * near + other_ref[piece(j), :]

        @pl.when(jnp.logical_not(last))
        def _():
            pass_on(j).start()

        hand_over(j, core).start()
        return carry

    lax.fori_loop(0, pieces, step, 0)

    def end(j, carry):
        swap(j).wait_send()

        @pl.when(jnp.logical_not(last))
        def _():
            pass_on(j).wait_send()

        hand_over(j, core).wait_send()
        hand_over(j, 1 - core).wait_recv()
        return carry

    lax.fori_loop(0, pieces, end, 0)


def chain(states, decay, chips, pieces):
    kinds, seqs, wide, state = states.shape
    own = states.reshape(kinds, seqs * wide, state)
    flat = (seqs * wide, state)
    out = pl.pallas_call(
        functools.partial(chain_kernel, chips, pieces),
        out_shape=jax.ShapeDtypeStruct(own.shape, F32),
        in_specs=[pl.BlockSpec(memory_space=VMEM)] * 2,
        out_specs=pl.BlockSpec(memory_space=VMEM),
        scratch_shapes=[VMEM(flat, F32), VMEM(decay.shape, F32), VMEM(flat, F32), VMEM(flat, F32)]
        + [DMA((pieces,)), DMA((pieces,)), DMA((1,)), DMA((1,))]
        + [DMA((pieces,))] * 4,
        compiler_params=pltpu.CompilerParams(collective_id=1, has_side_effects=True, vmem_limit_bytes=LIMIT),
    )(own, decay)
    return out.reshape(states.shape)


def back_kernel(
    lengths_ref, feat_ref, slope_ref, kq_ref, dt_ref, cum_ref, step_ref, og_ref, io_ref, x_ref, px_ref, wx_ref, sb_ref,
    dl_ref, skip_ref,
    mixed_ref, gx_ref, tail_ref, lead_ref, dstep_ref, dkq_ref, params_ref, ext_ref, dpre_ref,
):
    seq = pl.program_id(0)
    row_count, wide = feat_ref.shape[1:]
    edge, taps = px_ref.shape[1], wx_ref.shape[0]
    heads, state = step_ref.shape[2], kq_ref.shape[2] // 2
    valid = valid_rows(lengths_ref, seq, row_count)
    feat, kq, dt, cum = feat_ref[0], kq_ref[0], dt_ref[0], cum_ref[0]
    dy = og_ref[0].astype(F32) * valid
    dy_b = dy.astype(BF)
    feats, keys, queries = split(feat), split(kq[:, :state]), split(kq[:, state:])
    upper = triangle(row_count, True)
    ones = head_ones(wide, heads)
    lane = iota((1, wide), 1)
    row, col = iota((row_count, row_count), 0), iota((row_count, row_count), 1)
    causal = row >= col
    eye = jnp.where(row == col, 1.0, 0.0).astype(BF)

    cum_rows = mm_exact(split3(cum), eye, TN)
    dt_rows = mm_exact(split3(dt), eye, TN)
    scores = mm(queries, keys, NT)
    within = jnp.zeros((row_count, wide), F32)
    dfeat = jnp.zeros((row_count, wide), F32)
    dscores = jnp.zeros((row_count, row_count), F32)
    row_sums, col_sums = [], []
    for head in range(heads):
        gap = cum[:, head : head + 1] - cum_rows[head : head + 1, :]
        decays = jnp.where(causal, jnp.exp(jnp.where(causal, gap, 0.0)), 0.0)
        dt_row = dt_rows[head : head + 1, :]
        stepped = decays * dt_row
        mixing = stepped * scores
        here = (lane >= head * P_SIZE) & (lane < (head + 1) * P_SIZE)
        within = jnp.where(here, mm(split(mixing), feats, NN), within)
        dfeat = jnp.where(here, mm(split(mixing.T), (dy_b,), NN), dfeat)
        dmixing = mm((jnp.where(here, dy, 0.0).astype(BF),), feats, NT)
        dscores = dscores + dmixing * stepped
        row_sums.append(jnp.sum(dmixing * mixing, axis=1, keepdims=True))
        col_sums.append(jnp.sum(dmixing * decays * scores, axis=0, keepdims=True))

    incoming, later = io_ref[0, 0], io_ref[1, 0]
    incomings, laters = split(incoming), split(later)
    total = cum[row_count - 1 : row_count, :]
    left = jnp.exp(total - cum)
    weight = spread(left * dt, wide)
    grown = spread(jnp.exp(cum), wide)
    skip = spread(skip_ref[...], wide)
    carried = mm(queries, incomings, NT) * grown
    mixed_ref[0] = ((within + carried + skip * feat) * valid).astype(BF)
    back = mm(keys, laters, NT)
    dfeat = dfeat + skip * dy + weight * back
    grown_dy, weighted = split(grown * dy), split(weight * feat)
    dscores_s = split(dscores)
    dkq_ref[0, :, state:] = mm(dscores_s, keys, NN) + mm(grown_dy, incomings, NN)
    dkq_ref[0, :, :state] = mm(split(dscores.T), queries, NN) + mm(weighted, laters, NN)

    row_part = jnp.concatenate(row_sums, axis=1)
    col_part = jnp.concatenate(col_sums, axis=0)
    back_feat = mm_exact(split3(feat * back), ones, NN)
    dcum = row_part + mm_exact(split3(dy * carried), ones, NN) - back_feat * left * dt
    later_in = jnp.sum(mm_exact_left_t(ones, later * incoming), axis=1, keepdims=True)
    dtotal = jnp.sum(back_feat * left * dt, axis=0, keepdims=True)
    dtotal = dtotal + to_row(later_in, heads) * jnp.exp(total)
    drun = mm_exact_left(upper, split3(dcum), NN) - mm_exact_left(upper, split3(col_part * dt_rows), NT) + dtotal
    dsteps = mm_exact_left(eye, split3(col_part), NT) + back_feat * left
    rate = -jnp.exp(dl_ref[...])
    dstep = (dsteps + drun * rate) * valid * sigmoid(step_ref[0] + sb_ref[...])
    dstep_ref[0] = dstep
    ddecay = jnp.sum(drun * dt, axis=0, keepdims=True) * rate
    dskip = jnp.sum(mm_exact(split3(dy * feat), ones, NN), axis=0, keepdims=True)

    dpre = dfeat * slope_ref[0]
    lead_ref[0] = dpre[:8, :]
    dpre_ref[:row_count, :] = dpre
    dpre_ref[row_count:, :] = jnp.zeros((8, wide), F32)
    keep = jnp.where(lax.axis_index("inner") > 0, 1.0, 0.0)
    ext_ref[:edge, :] = px_ref[0].astype(F32) * keep
    ext_ref[edge:, :] = x_ref[0].astype(F32)
    wx = wx_ref[...]
    gx = jnp.zeros((row_count, wide), F32)
    for tap in range(taps):
        shift = taps - 1 - tap
        gx = gx + wx[tap : tap + 1] * dpre_ref[shift : shift + row_count, :]
    gx_ref[0] = gx.astype(BF)
    tail_ref[0] = gx[row_count - edge :, :]

    @pl.when(seq == 0)
    def _():
        params_ref[...] = jnp.zeros(params_ref.shape, F32)

    start = edge - (taps - 1)
    for tap in range(taps):
        params_ref[tap : tap + 1, :] += jnp.sum(
            dpre * ext_ref[start + tap : start + tap + row_count, :], axis=0, keepdims=True
        )
    params_ref[taps : taps + 1, :] += jnp.sum(dpre, axis=0, keepdims=True)
    params_ref[taps + 1 : taps + 2, :heads] += jnp.sum(dstep, axis=0, keepdims=True)
    params_ref[taps + 2 : taps + 3, :heads] += ddecay
    params_ref[taps + 3 : taps + 4, :heads] += dskip


def mm_exact_left_t(ones, a):
    out = None
    for part in split3(a):
        term = dot(ones, part, TN)
        out = term if out is None else out + term
    return out


def to_row(column, heads):
    same = iota((heads, heads), 0) == iota((heads, heads), 1)
    return jnp.sum(jnp.where(same, column, 0.0), axis=0, keepdims=True)


def back(lengths, feat, slope, kq, dt, cum, step_raw, output_grad, inout, x_raw, px, wx, sb, dl, skip):
    seqs, row_count, wide = x_raw.shape
    both, heads, edge = kq.shape[2], step_raw.shape[2], px.shape[1]
    state = both // 2

    def seq_block(*shape):
        return pl.BlockSpec((1,) + shape, lambda s: (s, 0, 0))

    def whole(a):
        return pl.BlockSpec(a.shape, lambda s: (0, 0))

    return pl.pallas_call(
        back_kernel,
        grid=(seqs,),
        out_shape=[
            jax.ShapeDtypeStruct((seqs, row_count, wide), BF),
            jax.ShapeDtypeStruct((seqs, row_count, wide), BF),
            jax.ShapeDtypeStruct((seqs, edge, wide), F32),
            jax.ShapeDtypeStruct((seqs, 8, wide), F32),
            jax.ShapeDtypeStruct((seqs, row_count, heads), F32),
            jax.ShapeDtypeStruct((seqs, row_count, both), F32),
            jax.ShapeDtypeStruct((8, wide), F32),
        ],
        in_specs=[
            pl.BlockSpec(memory_space=pltpu.SMEM),
            seq_block(row_count, wide), seq_block(row_count, wide), seq_block(row_count, both),
            seq_block(row_count, heads), seq_block(row_count, heads), seq_block(row_count, heads),
            seq_block(row_count, wide),
            pl.BlockSpec((2, 1, wide, state), lambda s: (0, s, 0, 0)),
            seq_block(row_count, wide), seq_block(edge, wide),
            whole(wx), whole(sb), whole(dl), whole(skip),
        ],
        out_specs=[
            seq_block(row_count, wide), seq_block(row_count, wide), seq_block(edge, wide), seq_block(8, wide),
            seq_block(row_count, heads), seq_block(row_count, both), pl.BlockSpec((8, wide), lambda s: (0, 0)),
        ],
        scratch_shapes=[VMEM((edge + row_count, wide), F32), VMEM((row_count + 8, wide), F32)],
        compiler_params=pltpu.CompilerParams(vmem_limit_bytes=LIMIT),
    )(lengths, feat, slope, kq, dt, cum, step_raw, output_grad, inout, x_raw, px, wx, sb, dl, skip)


def gather_sum_kernel(groups, size, part_ref, lead_ref, sum_ref, next_sum_ref, next_lead_ref, slots_ref,
                      send_a, recv_a, send_b, recv_b, send_e, recv_e):
    me, inner = lax.axis_index("outer"), lax.axis_index("inner")
    after, before = lax.rem(inner + 1, size), lax.rem(inner + size - 1, size)
    total_rows, width = part_ref.shape
    rows = total_rows // groups

    barrier = pltpu.get_barrier_semaphore()
    for other in (after, before):
        pl.semaphore_signal(barrier, inc=1, device_id={"inner": other}, device_id_type=MESH)

    def greet(d, carry):
        pl.semaphore_signal(
            barrier, inc=1, device_id={"outer": lax.rem(me + d, groups)}, device_id_type=MESH
        )
        return carry

    lax.fori_loop(1, groups, greet, 0)
    pl.semaphore_wait(barrier, groups + 1)

    def share(index):
        return pl.ds(pl.multiple_of(index * rows, rows), rows)

    def lead_copy():
        return pltpu.make_async_remote_copy(
            src_ref=lead_ref, dst_ref=next_lead_ref, send_sem=send_e.at[0], recv_sem=recv_e.at[0],
            device_id={"inner": before}, device_id_type=MESH,
        )

    def scatter(d):
        to = lax.rem(me + d, groups)
        return pltpu.make_async_remote_copy(
            src_ref=part_ref.at[share(to), :], dst_ref=slots_ref.at[d - 1], send_sem=send_a.at[d - 1],
            recv_sem=recv_a.at[d - 1], device_id={"outer": to}, device_id_type=MESH,
        )

    def gather(d):
        return pltpu.make_async_remote_copy(
            src_ref=sum_ref.at[share(me), :], dst_ref=sum_ref.at[share(me), :], send_sem=send_b.at[d - 1],
            recv_sem=recv_b.at[d - 1], device_id={"outer": lax.rem(me + d, groups)}, device_id_type=MESH,
        )

    def gathered(d):
        source = lax.rem(me + groups - d, groups)
        return pltpu.make_async_remote_copy(
            src_ref=sum_ref.at[share(source), :], dst_ref=sum_ref.at[share(source), :], send_sem=send_b.at[d - 1],
            recv_sem=recv_b.at[d - 1], device_id={"outer": source}, device_id_type=MESH,
        )

    def each(do):
        def body(d, carry):
            do(d)
            return carry

        lax.fori_loop(1, groups, body, 0)

    each(lambda d: scatter(d).start())
    lead_copy().start()
    each(lambda d: scatter(d).wait_recv())
    acc = part_ref[share(me), :]
    for d in range(groups - 1):
        acc = acc + slots_ref[d]
    sum_ref[share(me), :] = acc
    each(lambda d: gather(d).start())
    each(lambda d: gathered(d).wait_recv())

    seqs, lead = next_sum_ref.shape[:2]
    per_seq = total_rows // seqs
    rims = [
        pltpu.make_async_remote_copy(
            src_ref=sum_ref.at[pl.ds(s * per_seq, lead), :], dst_ref=next_sum_ref.at[s], send_sem=send_e.at[1 + s],
            recv_sem=recv_e.at[1 + s], device_id={"inner": before}, device_id_type=MESH,
        )
        for s in range(seqs)
    ]
    for copy in rims:
        copy.start()
    each(lambda d: scatter(d).wait_send())
    each(lambda d: gather(d).wait_send())
    lead_copy().wait()
    for copy in rims:
        copy.wait()


def gather_sum(parts, lead, groups, size):
    seqs, row_count, both = parts.shape
    flat = parts.reshape(seqs * row_count, both)
    rows = flat.shape[0] // groups
    total, next_sum, next_lead = pl.pallas_call(
        functools.partial(gather_sum_kernel, groups, size),
        out_shape=[
            jax.ShapeDtypeStruct(flat.shape, F32),
            jax.ShapeDtypeStruct((seqs, 8, both), F32),
            jax.ShapeDtypeStruct(lead.shape, F32),
        ],
        in_specs=[pl.BlockSpec(memory_space=VMEM)] * 2,
        out_specs=[pl.BlockSpec(memory_space=VMEM)] * 3,
        scratch_shapes=[VMEM((groups - 1, rows, both), F32)]
        + [DMA((groups - 1,))] * 4
        + [DMA((1 + seqs,))] * 2,
        compiler_params=pltpu.CompilerParams(collective_id=2, has_side_effects=True, vmem_limit_bytes=LIMIT),
    )(flat, lead)
    return total.reshape(parts.shape), next_sum, next_lead


def rows_kernel(
    dkq_ref, nsum_ref, bc_ref, pbc_ref, nbc_ref, wbc_ref, bbc_ref, nlead_ref, tail_ref, wx_ref, gx_in_ref,
    gbc_ref, params_ref, gx_ref, ext_ref, dpre_ref, pad_ref, *, size,
):
    seq = pl.program_id(0)
    row_count, both = bc_ref.shape[1:]
    edge, taps, lead = pbc_ref.shape[1], wbc_ref.shape[0], nsum_ref.shape[1]
    state = both // 2
    inner = lax.axis_index("inner")
    has_before = jnp.where(inner > 0, 1.0, 0.0)
    has_after = jnp.where(inner < size - 1, 1.0, 0.0)
    ext_ref[:edge, :] = pbc_ref[0].astype(F32) * has_before
    ext_ref[edge : edge + row_count, :] = bc_ref[0].astype(F32)
    ext_ref[edge + row_count :, :] = nbc_ref[0].astype(F32)
    start = edge - (taps - 1)
    wbc, wx = wbc_ref[...], wx_ref[...]
    pre = convolved(ext_ref, start, wbc, bbc_ref[...], row_count + lead)
    gate = sigmoid(pre)
    slope = gate * (1.0 + pre * (1.0 - gate))
    dpre_ref[:row_count, :] = dkq_ref[0] * slope[:row_count, :]
    dpre_ref[row_count:, :] = nsum_ref[0] * slope[row_count:, :] * has_after
    grad = jnp.zeros((row_count, both), F32)
    for tap in range(taps):
        shift = taps - 1 - tap
        grad = grad + wbc[tap : tap + 1] * dpre_ref[shift : shift + row_count, :]
    gbc_ref[0] = grad.astype(BF)

    @pl.when(seq == 0)
    def _():
        params_ref[...] = jnp.zeros(params_ref.shape, F32)

    dpre = dpre_ref[:row_count, :]
    for tap in range(taps + 1):
        term = dpre if tap == taps else dpre * ext_ref[start + tap : start + tap + row_count, :]
        term = jnp.sum(term, axis=0, keepdims=True)
        params_ref[tap : tap + 1, :] += term[:, :state]
        params_ref[8 + tap : 9 + tap, :] += term[:, state:]

    wide = tail_ref.shape[2]
    pad_ref[:edge, :] = jnp.zeros((edge, wide), F32)
    pad_ref[edge : edge + lead, :] = nlead_ref[0] * has_after
    tail = tail_ref[0]
    for tap in range(taps):
        shift = taps - 1 - tap
        tail = tail + wx[tap : tap + 1] * pad_ref[shift : shift + edge, :]
    gx_ref[0] = tail.astype(BF)


def bc_rows(dkq, nsum, bc_raw, pbc, nbc, wbc, bbc, nlead, tail, wx, gx, size):
    seqs, row_count, both = bc_raw.shape
    edge, wide, lead = pbc.shape[1], gx.shape[2], nsum.shape[1]
    state = both // 2

    def seq_block(*shape):
        return pl.BlockSpec((1,) + shape, lambda s: (s, 0, 0))

    def whole(a):
        return pl.BlockSpec(a.shape, lambda s: (0, 0))

    last = row_count // edge - 1
    return pl.pallas_call(
        functools.partial(rows_kernel, size=size),
        grid=(seqs,),
        out_shape=[
            jax.ShapeDtypeStruct((seqs, row_count, both), BF),
            jax.ShapeDtypeStruct((16, state), F32),
            jax.ShapeDtypeStruct(gx.shape, BF),
        ],
        in_specs=[
            seq_block(row_count, both), seq_block(lead, both), seq_block(row_count, both), seq_block(edge, both),
            seq_block(edge, both), whole(wbc), whole(bbc), seq_block(lead, wide), seq_block(edge, wide), whole(wx),
            pl.BlockSpec(memory_space=pl.ANY),
        ],
        out_specs=[
            seq_block(row_count, both),
            pl.BlockSpec((16, state), lambda s: (0, 0)),
            pl.BlockSpec((1, edge, wide), lambda s: (s, last, 0)),
        ],
        input_output_aliases={10: 2},
        scratch_shapes=[
            VMEM((edge + row_count + edge, both), F32), VMEM((row_count + lead, both), F32), VMEM((edge + lead, wide), F32)
        ],
        compiler_params=pltpu.CompilerParams(vmem_limit_bytes=LIMIT),
    )(dkq, nsum, bc_raw, pbc, nbc, wbc, bbc, nlead, tail, wx, gx)


def params_kernel(group, count, px_ref, pbc_ref, wx_out, bx_out, wbc_out, bbc_out, sb_out, dl_out, skip_out,
                  mine_ref, mate_ref, near_ref, far_ref, send_sem, recv_sem):
    me = lax.axis_index("inner")
    chip, core = me // 2, lax.rem(me, 2)
    block, spot = chip // group, lax.rem(chip, group)

    def near_peer(d):
        return (block * group + lax.rem(spot + d, group)) * 2 + core

    def far_peer(d):
        return (lax.rem(block + d, count) * group + spot) * 2 + core

    mate = chip * 2 + 1 - core
    peers = [mate] + [near_peer(d) for d in range(1, group)] + [far_peer(d) for d in range(1, count)]
    barrier = pltpu.get_barrier_semaphore()
    for other in peers:
        pl.semaphore_signal(barrier, inc=1, device_id={"inner": other}, device_id_type=MESH)
    pl.semaphore_wait(barrier, len(peers))

    def remote(src, dst, i, other):
        return pltpu.make_async_remote_copy(
            src_ref=src, dst_ref=dst, send_sem=send_sem.at[i], recv_sem=recv_sem.at[i],
            device_id={"inner": other}, device_id_type=MESH,
        )

    head_rows = px_ref.shape[0]
    mine_ref[:head_rows, :] = px_ref[...]
    mine_ref[head_rows:, :] = pbc_ref[...]
    copy = remote(mine_ref, mate_ref, 0, mate)
    copy.start()
    copy.wait()
    near_ref[spot] = mine_ref[...] + mate_ref[...]

    def stage(buf, index, many, peer, first_sem):
        copies = []
        for d in range(1, many):
            copies.append(remote(buf.at[index], buf.at[index], first_sem + d - 1, peer(d)))
            copies[-1].start()
        for d in range(1, many):
            source = lax.rem(index + many - d, many)
            remote(buf.at[source], buf.at[source], first_sem + d - 1, peer(d)).wait_recv()
        for c in copies:
            c.wait_send()
        total = buf[0]
        for k in range(1, many):
            total = total + buf[k]
        return total

    far_ref[block] = stage(near_ref, spot, group, near_peer, 1)
    total = stage(far_ref, block, count, far_peer, group)
    taps, heads, state = wx_out.shape[0], sb_out.shape[1], px_ref.shape[1]
    wx_out[...] = total[:taps]
    bx_out[...] = total[taps : taps + 1]
    sb_out[...] = total[taps + 1 : taps + 2, :heads]
    dl_out[...] = total[taps + 2 : taps + 3, :heads]
    skip_out[...] = total[taps + 3 : taps + 4, :heads]
    wbc_out[:, :state] = total[head_rows : head_rows + taps]
    wbc_out[:, state:] = total[head_rows + 8 : head_rows + 8 + taps]
    bbc_out[:, :state] = total[head_rows + taps : head_rows + taps + 1]
    bbc_out[:, state:] = total[head_rows + 8 + taps : head_rows + 9 + taps]


def sum_params(px, pbc, taps, heads, chips):
    group = 4 if chips % 4 == 0 else 1
    count = chips // group
    width = px.shape[1]
    shape = (px.shape[0] + pbc.shape[0], width)
    return pl.pallas_call(
        functools.partial(params_kernel, group, count),
        out_shape=[
            jax.ShapeDtypeStruct(s, F32)
            for s in ((taps, width), (1, width), (taps, 2 * width), (1, 2 * width), (1, heads), (1, heads), (1, heads))
        ],
        in_specs=[pl.BlockSpec(memory_space=VMEM)] * 2,
        out_specs=[pl.BlockSpec(memory_space=VMEM)] * 7,
        scratch_shapes=[
            VMEM(shape, F32), VMEM(shape, F32), VMEM((group,) + shape, F32), VMEM((count,) + shape, F32),
            DMA((group + count,)), DMA((group + count,)),
        ],
        compiler_params=pltpu.CompilerParams(collective_id=3, has_side_effects=True),
    )(px, pbc)


def per_device(
    sizes, x_raw, bc_raw, step_raw, lengths, conv_weight_x, conv_bias_x, conv_weight_bc, conv_bias_bc, step_bias,
    decay_log, skip_gain, output_grad,
):
    groups, size = sizes
    edge, taps, heads = 16, conv_weight_x.shape[0], step_raw.shape[2]
    bx, bbc = conv_bias_x[None], conv_bias_bc[None]
    sb, dl, skip = step_bias[None], decay_log[None], skip_gain[None]
    px, pbc, nbc = edges(x_raw, bc_raw, size, edge)
    states, decay, feat, slope, kq, dt, cum = front(
        lengths, x_raw, bc_raw, px, pbc, step_raw, output_grad, conv_weight_x, bx, conv_weight_bc, bbc, sb, dl
    )
    inout = chain(states, decay, size // 2, 16)
    mixed, gx, tail, lead, dstep, dkq, px_sums = back(
        lengths, feat, slope, kq, dt, cum, step_raw, output_grad, inout, x_raw, px, conv_weight_x, sb, dl, skip
    )
    dkq_sum, nsum, nlead = gather_sum(dkq, lead, groups, size)
    gbc, pbc_sums, gx = bc_rows(
        dkq_sum, nsum, bc_raw, pbc, nbc, conv_weight_bc, bbc, nlead, tail, conv_weight_x, gx, size
    )
    wx, bx_g, wbc, bbc_g, sb_g, dl_g, skip_g = sum_params(px_sums, pbc_sums, taps, heads, size // 2)
    return (mixed, gx, gbc, dstep, wx, bx_g[0], wbc, bbc_g[0], sb_g[0], dl_g[0], skip_g[0])


def solution(mesh):
    rows_and_heads = P(None, "inner", "outer")
    return jax.shard_map(
        functools.partial(per_device, (mesh.shape["outer"], mesh.shape["inner"])),
        mesh=mesh,
        in_specs=(
            rows_and_heads, P(None, "inner", None), rows_and_heads, P(), P(None, "outer"), P("outer"), P(), P(),
            P("outer"), P("outer"), P("outer"), rows_and_heads,
        ),
        out_specs=(
            rows_and_heads, rows_and_heads, P(None, "inner", None), rows_and_heads, P(None, "outer"), P("outer"), P(),
            P(), P("outer"), P("outer"), P("outer"),
        ),
        check_vma=False,
    )
```

```python
import functools

import jax
import jax.numpy as jnp
from jax import lax
from jax.experimental import pallas as pl
from jax.experimental.pallas import tpu as pltpu
from jax.sharding import PartitionSpec as P

P_SIZE = 64
F32 = jnp.float32
BF = jnp.bfloat16
MESH = pl.DeviceIdType.MESH
VMEM = pltpu.VMEM
DMA = pltpu.SemaphoreType.DMA
LIMIT = 48 * 1024 * 1024
NN = ((1,), (0,))
NT = ((1,), (1,))
TN = ((0,), (0,))


def dot(a, b, dims):
    return lax.dot_general(a, b, (dims, ((), ())), preferred_element_type=F32)


def split(a):
    high = a.astype(BF)
    return high, (a - high.astype(F32)).astype(BF)


def split3(a):
    high = a.astype(BF)
    rest = a - high.astype(F32)
    mid = rest.astype(BF)
    return high, mid, (rest - mid.astype(F32)).astype(BF)


def mm(a, b, dims):
    out = dot(a[0], b[0], dims)
    if len(b) > 1:
        out = out + dot(a[0], b[1], dims)
    if len(a) > 1:
        out = out + dot(a[1], b[0], dims)
    return out


def mm_exact(parts, ones, dims):
    out = dot(parts[0], ones, dims)
    for part in parts[1:]:
        out = out + dot(part, ones, dims)
    return out


def mm_exact_left(ones, parts, dims):
    out = dot(ones, parts[0], dims)
    for part in parts[1:]:
        out = out + dot(ones, part, dims)
    return out


def iota(shape, dim):
    return lax.broadcasted_iota(jnp.int32, shape, dim)


def head_ones(heads, width):
    row, col = iota((heads, width), 0), iota((heads, width), 1)
    return jnp.where((col >= row * P_SIZE) & (col < (row + 1) * P_SIZE), 1.0, 0.0).astype(BF)


def spread(per_head, ones):
    return mm_exact(split3(per_head), ones, TN)


def head_sums(a, ones):
    return mm_exact_left(ones, split3(a), NT)


def columns(per_head, eye):
    return mm_exact_left(eye, split3(per_head), NT)


def to_row(column):
    heads = column.shape[0]
    same = iota((heads, heads), 0) == iota((heads, heads), 1)
    return jnp.sum(jnp.where(same, column, 0.0), axis=0, keepdims=True)


def scalars(ref, shape, dim, each):
    place = iota(shape, dim)
    out = jnp.full(shape, ref[0], F32)
    for i in range(1, ref.shape[0]):
        out = jnp.where(place >= i * each, ref[i], out)
    return out


def triangle(rows, upper):
    row, col = iota((rows, rows), 0), iota((rows, rows), 1)
    return jnp.where(col >= row if upper else row >= col, 1.0, 0.0).astype(BF)


def convolved(ext_ref, start, weight, bias, row_count):
    pre_act = bias
    for tap in range(weight.shape[0]):
        pre_act = pre_act + weight[tap : tap + 1] * ext_ref[start + tap : start + tap + row_count, :]
    return pre_act


def softplus(z):
    return jnp.maximum(z, 0.0) + jnp.log1p(jnp.exp(-jnp.abs(z)))


def sigmoid(z):
    return 1.0 / (1.0 + jnp.exp(-z))


def valid_rows(lengths_ref, seq, row_count, dim):
    first = lax.axis_index("inner") * row_count
    shape = (row_count, 1) if dim == 0 else (1, row_count)
    return jnp.where(first + iota(shape, dim) < lengths_ref[seq], 1.0, 0.0)


def remote(src, dst, send, recv, **where):
    return pltpu.make_async_remote_copy(
        src_ref=src, dst_ref=dst, send_sem=send, recv_sem=recv, device_id=where, device_id_type=MESH
    )


def greet(**where):
    pl.semaphore_signal(pltpu.get_barrier_semaphore(), inc=1, device_id=where, device_id_type=MESH)


def loop(first, count, do):
    def body(i, carry):
        do(i)
        return carry

    lax.fori_loop(first, count, body, 0)


def states_kernel(
    size, pieces,
    lengths_ref, sb_ref, dl_ref, x_ref, bc_ref, step_ref, og_ref, wx_ref, bx_ref, wbc_ref, bbc_ref,
    out_ref, feat_ref, slope_ref, kq_ref, slope_bc_ref, dt_ref, cum_ref, px_ref, pbc_ref, nbc_ref,
    extx_ref, extbc_ref, own_ref, other_ref, decay_ref, odecay_ref, far_ref, near_ref,
    esend, erecv, psend, precv, fsend, frecv, nsend, nrecv,
):
    seqs, row_count, wide = x_ref.shape
    edge, taps, heads = px_ref.shape[1], wx_ref.shape[0], step_ref.shape[1]
    state = wbc_ref.shape[1] // 2
    chips = size // 2
    me = lax.axis_index("inner")
    after, before = lax.rem(me + 1, size), lax.rem(me + size - 1, size)
    chip, core = me // 2, lax.rem(me, 2)
    mate = chip * 2 + 1 - core
    ahead = lax.rem(chip + 1 - 2 * core + chips, chips) * 2 + core
    behind = lax.rem(chip - 1 + 2 * core + chips, chips) * 2 + core
    place = jnp.where(core == 0, chip, chips - 1 - chip)
    first, last = place == 0, place == chips - 1

    peers = (after, before, mate, ahead, behind)
    for other in peers:
        greet(inner=other)
    pl.semaphore_wait(pltpu.get_barrier_semaphore(), len(peers))

    tail = pl.ds(row_count - edge, edge)
    rims = [
        remote(x_ref.at[:, tail, :], px_ref, esend.at[0], erecv.at[0], inner=after),
        remote(bc_ref.at[:, tail, :], pbc_ref, esend.at[1], erecv.at[1], inner=after),
        remote(bc_ref.at[:, pl.ds(0, edge), :], nbc_ref, esend.at[2], erecv.at[2], inner=before),
    ]
    for copy in rims:
        copy.start()

    rows = seqs * wide // pieces
    per_head, per_seq = P_SIZE // rows, wide // rows

    def piece(j):
        return pl.ds(pl.multiple_of(j * rows, rows), rows)

    def swap(j):
        return remote(own_ref.at[1 - core, piece(j), :], other_ref.at[piece(j), :], psend.at[j], precv.at[j], inner=mate)

    def pass_on(j):
        return remote(far_ref.at[piece(j), :], out_ref.at[core, piece(j), :], fsend.at[j], frecv.at[j], inner=ahead)

    def hand_over(j, slot):
        return remote(near_ref.at[piece(j), :], out_ref.at[slot, piece(j), :], nsend.at[j], nrecv.at[j], inner=mate)

    ones = head_ones(heads, wide)
    upper = triangle(row_count, True)
    rate = -jnp.exp(scalars(dl_ref, (heads, 1), 0, 1))
    bias = scalars(sb_ref, (heads, 1), 0, 1)
    for seq in range(seqs):
        dt = softplus(step_ref[seq] + bias) * valid_rows(lengths_ref, seq, row_count, 1)
        cum = mm_exact(split3(dt * rate), upper, NN)
        dt_ref[seq] = dt
        cum_ref[seq] = cum
        decay_ref[seq] = jnp.broadcast_to(jnp.exp(cum[:, row_count - 1 :]), (heads, state))
    decays = remote(decay_ref, odecay_ref, esend.at[3], erecv.at[3], inner=mate)
    decays.start()

    keep = jnp.where(me > 0, 1.0, 0.0)
    start = edge - (taps - 1)
    for copy in rims:
        copy.wait_recv()
    for seq in range(seqs):
        extx_ref[:edge, :] = px_ref[seq].astype(F32) * keep
        extx_ref[edge:, :] = x_ref[seq].astype(F32)
        extbc_ref[:edge, :] = pbc_ref[seq].astype(F32) * keep
        extbc_ref[edge:, :] = bc_ref[seq].astype(F32)
        pre_x = convolved(extx_ref, start, wx_ref[...], bx_ref[...], row_count)
        gate = sigmoid(pre_x)
        feat = pre_x * gate
        feat_ref[seq] = feat
        slope_ref[seq] = gate * (1.0 + pre_x * (1.0 - gate))
        pre_bc = convolved(extbc_ref, start, wbc_ref[...], bbc_ref[...], row_count)
        gate = sigmoid(pre_bc)
        kq = pre_bc * gate
        kq_ref[seq] = kq
        slope_bc_ref[seq] = gate * (1.0 + pre_bc * (1.0 - gate))
        dt, cum = dt_ref[seq], cum_ref[seq]
        weight = spread(jnp.exp(cum[:, row_count - 1 :] - cum) * dt, ones)
        grown = spread(jnp.exp(cum), ones)
        dy = og_ref[seq].astype(F32) * valid_rows(lengths_ref, seq, row_count, 0)
        keys, queries = split(kq[:, :state]), split(kq[:, state:])
        own_ref[0, seq * wide : (seq + 1) * wide, :] = mm(split(weight * feat), keys, TN)
        own_ref[1, seq * wide : (seq + 1) * wide, :] = mm(split(grown * dy), queries, TN)
        loop(seq * per_seq, (seq + 1) * per_seq, lambda j: swap(j).start())
    decays.wait()

    def seq_head(j):
        head = j // per_head
        return head // heads, pl.ds(lax.rem(head, heads), 1)

    def join(j):
        seq, head = seq_head(j)
        swap(j).wait_recv()
        far_ref[piece(j), :] = odecay_ref[seq, head, :] * own_ref[core, piece(j), :] + other_ref[piece(j), :]

    loop(0, pieces, join)

    @pl.when(first)
    def _():
        out_ref[core] = jnp.zeros((seqs * wide, state), F32)

    def step(j):
        seq, head = seq_head(j)

        @pl.when(jnp.logical_not(first))
        def _():
            pass_on(j).wait_recv()

        carried = out_ref[core, piece(j), :]
        near = decay_ref[seq, head, :]

        @pl.when(jnp.logical_not(last))
        def _():
            far_ref[piece(j), :] = near * odecay_ref[seq, head, :] * carried + far_ref[piece(j), :]
            pass_on(j).start()

        near_ref[piece(j), :] = near * carried + own_ref[core, piece(j), :]
        hand_over(j, core).start()

    loop(0, pieces, step)

    def end(j):
        swap(j).wait_send()

        @pl.when(jnp.logical_not(last))
        def _():
            pass_on(j).wait_send()

        hand_over(j, core).wait_send()
        hand_over(j, 1 - core).wait_recv()

    loop(0, pieces, end)
    for copy in rims:
        copy.wait_send()


def states(lengths, sb, dl, x_raw, bc_raw, step, output_grad, wx, bx, wbc, bbc, size, edge, pieces):
    seqs, row_count, wide = x_raw.shape
    both, heads = bc_raw.shape[2], step.shape[1]
    state = both // 2
    flat = (seqs * wide, state)
    vmem, smem = pl.BlockSpec(memory_space=VMEM), pl.BlockSpec(memory_space=pltpu.SMEM)
    return pl.pallas_call(
        functools.partial(states_kernel, size, pieces),
        name="states",
        out_shape=[
            jax.ShapeDtypeStruct((2,) + flat, F32),
            jax.ShapeDtypeStruct((seqs, row_count, wide), F32),
            jax.ShapeDtypeStruct((seqs, row_count, wide), F32),
            jax.ShapeDtypeStruct((seqs, row_count, both), F32),
            jax.ShapeDtypeStruct((seqs, row_count, both), F32),
            jax.ShapeDtypeStruct((seqs, heads, row_count), F32),
            jax.ShapeDtypeStruct((seqs, heads, row_count), F32),
            jax.ShapeDtypeStruct((seqs, edge, wide), BF),
            jax.ShapeDtypeStruct((seqs, edge, both), BF),
            jax.ShapeDtypeStruct((seqs, edge, both), BF),
        ],
        in_specs=[smem] * 3 + [vmem] * 8,
        out_specs=[vmem] * 10,
        scratch_shapes=[
            VMEM((edge + row_count, wide), F32), VMEM((edge + row_count, both), F32),
            VMEM((2,) + flat, F32), VMEM(flat, F32), VMEM((seqs, heads, state), F32), VMEM((seqs, heads, state), F32),
            VMEM(flat, F32), VMEM(flat, F32),
            DMA((4,)), DMA((4,)),
        ] + [DMA((pieces,))] * 6,
        compiler_params=pltpu.CompilerParams(collective_id=0, has_side_effects=True, vmem_limit_bytes=LIMIT),
    )(lengths, sb, dl, x_raw, bc_raw, step, output_grad, wx, bx, wbc, bbc)


def back_one(
    seq, lengths_ref, sb_ref, dl_ref, skip_ref, feat_ref, slope_ref, kq_ref, dt_ref, cum_ref, step_ref, og_ref, io_ref,
    x_ref, px_ref, wx_ref,
    mixed_ref, gx_ref, dstep_ref, dkq_ref, lead_ref, params_ref, ext_ref, dpre_ref,
):
    row_count, wide = feat_ref.shape[1:]
    edge, taps = px_ref.shape[1], wx_ref.shape[0]
    heads, state = step_ref.shape[1], kq_ref.shape[2] // 2
    valid = valid_rows(lengths_ref, seq, row_count, 0)
    feat, kq, dt, cum = feat_ref[seq], kq_ref[seq], dt_ref[seq], cum_ref[seq]
    dy = og_ref[seq].astype(F32) * valid
    dy_b = dy.astype(BF)
    feats, keys, queries = split(feat), split(kq[:, :state]), split(kq[:, state:])
    ones = head_ones(heads, wide)
    lane = iota((1, wide), 1)
    row, col = iota((row_count, row_count), 0), iota((row_count, row_count), 1)
    causal = row >= col
    eye = jnp.where(row == col, 1.0, 0.0).astype(BF)
    cum_cols = columns(cum, eye)

    scores = mm(queries, keys, NT)
    within = jnp.zeros((row_count, wide), F32)
    dfeat = jnp.zeros((row_count, wide), F32)
    dscores = jnp.zeros((row_count, row_count), F32)
    row_sums, col_sums = [], []
    for head in range(heads):
        gap = cum_cols[:, head : head + 1] - cum[head : head + 1, :]
        decays = jnp.where(causal, jnp.exp(jnp.where(causal, gap, 0.0)), 0.0)
        stepped = decays * dt[head : head + 1, :]
        mixing = stepped * scores
        here = (lane >= head * P_SIZE) & (lane < (head + 1) * P_SIZE)
        within = jnp.where(here, mm(split(mixing), feats, NN), within)
        dfeat = jnp.where(here, mm(split(mixing.T), (dy_b,), NN), dfeat)
        dmixing = mm((jnp.where(here, dy, 0.0).astype(BF),), feats, NT)
        dscores = dscores + dmixing * stepped
        row_sums.append(jnp.sum(dmixing * mixing, axis=1, keepdims=True))
        col_sums.append(jnp.sum(dmixing * decays * scores, axis=0, keepdims=True))

    block = pl.ds(seq * wide, wide)
    incoming, later = io_ref[0, block, :], io_ref[1, block, :]
    incomings, laters = split(incoming), split(later)
    total = cum[:, row_count - 1 :]
    left = jnp.exp(total - cum)
    weight = spread(left * dt, ones)
    grown = spread(jnp.exp(cum), ones)
    skip = scalars(skip_ref, (1, wide), 1, P_SIZE)
    carried = mm(queries, incomings, NT) * grown
    mixed_ref[seq] = ((within + carried + skip * feat) * valid).astype(BF)
    back = mm(keys, laters, NT)
    dfeat = dfeat + skip * dy + weight * back
    grown_dy, weighted = split(grown * dy), split(weight * feat)
    rows = pl.ds(seq * row_count, row_count)
    dkq_ref[rows, state:] = mm(split(dscores), keys, NN) + mm(grown_dy, incomings, NN)
    dkq_ref[rows, :state] = mm(split(dscores.T), queries, NN) + mm(weighted, laters, NN)

    row_part = mm_exact(split3(jnp.concatenate(row_sums, axis=1)), eye, TN)
    col_part = jnp.concatenate(col_sums, axis=0)
    back_left = head_sums(feat * back, ones) * left
    dcum = row_part + head_sums(dy * carried, ones) - (col_part + back_left) * dt
    later_in = jnp.sum(mm_exact_left(ones, split3(later * incoming), NN), axis=1, keepdims=True)
    dtotal = jnp.sum(back_left * dt, axis=1, keepdims=True) + later_in * jnp.exp(total)
    drun = mm_exact(split3(dcum), triangle(row_count, False), NN) + dtotal
    rate = -jnp.exp(scalars(dl_ref, (heads, 1), 0, 1))
    z = step_ref[seq] + scalars(sb_ref, (heads, 1), 0, 1)
    dstep = (col_part + back_left + drun * rate) * valid_rows(lengths_ref, seq, row_count, 1) * sigmoid(z)
    dstep_ref[seq] = dstep
    ddecay = jnp.sum(drun * dt, axis=1, keepdims=True) * rate
    dskip = jnp.sum(head_sums(dy * feat, ones), axis=1, keepdims=True)

    dpre = dfeat * slope_ref[seq]
    lead_ref[seq] = dpre[:8, :]
    dpre_ref[:row_count, :] = dpre
    dpre_ref[row_count:, :] = jnp.zeros((8, wide), F32)
    keep = jnp.where(lax.axis_index("inner") > 0, 1.0, 0.0)
    ext_ref[:edge, :] = px_ref[seq].astype(F32) * keep
    ext_ref[edge:, :] = x_ref[seq].astype(F32)
    wx = wx_ref[...]
    gx = jnp.zeros((row_count, wide), F32)
    for tap in range(taps):
        shift = taps - 1 - tap
        gx = gx + wx[tap : tap + 1] * dpre_ref[shift : shift + row_count, :]
    gx_ref[seq] = gx

    start = edge - (taps - 1)
    for tap in range(taps):
        term = dpre * ext_ref[start + tap : start + tap + row_count, :]
        params_ref[tap : tap + 1, :] += jnp.sum(term, axis=0, keepdims=True)
    params_ref[taps : taps + 1, :] += jnp.sum(dpre, axis=0, keepdims=True)
    for i, part in enumerate((jnp.sum(dstep, axis=1, keepdims=True), ddecay, dskip)):
        params_ref[taps + 1 + i : taps + 2 + i, :heads] += to_row(part)


def back_kernel(
    groups, size, near,
    lengths_ref, sb_ref, dl_ref, skip_ref, feat_ref, slope_ref, kq_ref, slope_bc_ref, dt_ref, cum_ref, step_ref, og_ref,
    io_ref, x_ref, px_ref, bc_ref, pbc_ref, wx_ref,
    mixed_ref, gx_ref, dstep_ref, sum_ref, next_sum_ref, next_lead_ref, px_out, pbc_out,
    ext_ref, dpre_ref, extbc_ref, dkq_ref, lead_ref, slots_ref, mine_ref, mate_ref, near_ref, far_ref, outer_ref,
    send_a, recv_a, send_b, recv_b, send_c, recv_c, send_e, recv_e, send_p, recv_p,
):
    me, inner = lax.axis_index("outer"), lax.axis_index("inner")
    after, before = lax.rem(inner + 1, size), lax.rem(inner + size - 1, size)
    chip, core = inner // 2, lax.rem(inner, 2)
    mate = chip * 2 + 1 - core
    chips = size // 2
    blocks = chips // near
    block, spot = chip // near, lax.rem(chip, near)

    def near_peer(d):
        return (block * near + lax.rem(spot + d, near)) * 2 + core

    def far_peer(d):
        return (lax.rem(block + d, blocks) * near + spot) * 2 + core

    peers = [after, before, mate] + [near_peer(d) for d in range(1, near)] + [far_peer(d) for d in range(1, blocks)]
    for other in peers:
        greet(inner=other)
    loop(1, groups, lambda d: greet(outer=lax.rem(me + d, groups)))

    seqs, row_count, both = kq_ref.shape
    state, head_rows = both // 2, px_out.shape[0]
    edge, taps = px_ref.shape[1], wx_ref.shape[0]
    mine_ref[...] = jnp.zeros(mine_ref.shape, F32)
    for seq in range(seqs):
        back_one(
            seq, lengths_ref, sb_ref, dl_ref, skip_ref, feat_ref, slope_ref, kq_ref, dt_ref, cum_ref, step_ref, og_ref,
            io_ref, x_ref, px_ref, wx_ref,
            mixed_ref, gx_ref, dstep_ref, dkq_ref, lead_ref, mine_ref, ext_ref, dpre_ref,
        )

    pl.semaphore_wait(pltpu.get_barrier_semaphore(), len(peers) + groups - 1)

    rows = seqs * row_count // groups

    def share(index):
        return pl.ds(pl.multiple_of(index * rows, rows), rows)

    def scatter(d):
        to = lax.rem(me + d, groups)
        return remote(
            dkq_ref.at[share(to), :], slots_ref.at[d - 1], send_a.at[d - 1], recv_a.at[d - 1], outer=to
        )

    def gather(d, source):
        part = sum_ref.at[share(source), :]
        return remote(part, part, send_b.at[d - 1], recv_b.at[d - 1], outer=lax.rem(me + d, groups))

    def gather_params(d, source):
        part = outer_ref.at[source]
        return remote(part, part, send_c.at[d - 1], recv_c.at[d - 1], outer=lax.rem(me + d, groups))

    def source(d):
        return lax.rem(me + groups - d, groups)

    loop(1, groups, lambda d: scatter(d).start())
    lead_copy = remote(lead_ref, next_lead_ref, send_e.at[0], recv_e.at[0], inner=before)
    lead_copy.start()

    keep = jnp.where(inner > 0, 1.0, 0.0)
    start = edge - (taps - 1)
    for seq in range(seqs):
        extbc_ref[:edge, :] = pbc_ref[seq].astype(F32) * keep
        extbc_ref[edge:, :] = bc_ref[seq].astype(F32)
        dpre = dkq_ref[seq * row_count : (seq + 1) * row_count, :] * slope_bc_ref[seq]
        for tap in range(taps + 1):
            term = dpre if tap == taps else dpre * extbc_ref[start + tap : start + tap + row_count, :]
            term = jnp.sum(term, axis=0, keepdims=True)
            mine_ref[head_rows + tap : head_rows + tap + 1, :] += term[:, :state]
            mine_ref[head_rows + 8 + tap : head_rows + 9 + tap, :] += term[:, state:]

    mate_copy = remote(mine_ref, mate_ref, send_p.at[0], recv_p.at[0], inner=mate)
    mate_copy.start()
    mate_copy.wait()

    def stage(buf, index, many, peer, first_sem):
        for d in range(1, many):
            remote(buf.at[index], buf.at[index], send_p.at[first_sem + d], recv_p.at[first_sem + d], inner=peer(d)).start()

        def finish():
            for d in range(1, many):
                part = buf.at[lax.rem(index + many - d, many)]
                remote(part, part, send_p.at[first_sem + d], recv_p.at[first_sem + d], inner=peer(d)).wait_recv()
                remote(part, part, send_p.at[first_sem + d], recv_p.at[first_sem + d], inner=peer(d)).wait_send()
            total = buf[0]
            for k in range(1, many):
                total = total + buf[k]
            return total

        return finish

    near_ref[spot] = mine_ref[...] + mate_ref[...]
    finish_near = stage(near_ref, spot, near, near_peer, 0)
    far_ref[block] = finish_near()
    finish_far = stage(far_ref, block, blocks, far_peer, near)

    loop(1, groups, lambda d: scatter(d).wait_recv())
    acc = dkq_ref[share(me), :]
    for d in range(groups - 1):
        acc = acc + slots_ref[d]
    sum_ref[share(me), :] = acc
    loop(1, groups, lambda d: gather(d, me).start())

    total = finish_far()
    px_out[...] = total[:head_rows]
    outer_ref[me] = total[head_rows:]
    loop(1, groups, lambda d: gather_params(d, me).start())

    loop(1, groups, lambda d: gather(d, source(d)).wait_recv())
    lead = next_sum_ref.shape[1]
    rims = [
        remote(
            sum_ref.at[pl.ds(s * row_count, lead), :], next_sum_ref.at[s], send_e.at[1 + s], recv_e.at[1 + s], inner=before
        )
        for s in range(seqs)
    ]
    for copy in rims:
        copy.start()
    loop(1, groups, lambda d: gather_params(d, source(d)).wait_recv())
    total = outer_ref[0]
    for k in range(1, groups):
        total = total + outer_ref[k]
    pbc_out[...] = total

    def drain(d):
        scatter(d).wait_send()
        gather(d, me).wait_send()
        gather_params(d, me).wait_send()

    loop(1, groups, drain)
    lead_copy.wait()
    for copy in rims:
        copy.wait()


def back(
    lengths, sb, dl, skip, feat, slope, kq, slope_bc, dt, cum, step, output_grad, inout, x_raw, px, bc_raw, pbc, wx,
    groups, size,
):
    seqs, row_count, wide = x_raw.shape
    both, heads, edge = kq.shape[2], step.shape[1], px.shape[1]
    state, chips = both // 2, size // 2
    near = 4 if chips % 4 == 0 else 1
    rows = seqs * row_count // groups
    sums = (24, state)
    vmem, smem = pl.BlockSpec(memory_space=VMEM), pl.BlockSpec(memory_space=pltpu.SMEM)
    return pl.pallas_call(
        functools.partial(back_kernel, groups, size, near),
        name="back",
        out_shape=[
            jax.ShapeDtypeStruct((seqs, row_count, wide), BF),
            jax.ShapeDtypeStruct((seqs, row_count, wide), F32),
            jax.ShapeDtypeStruct((seqs, heads, row_count), F32),
            jax.ShapeDtypeStruct((seqs * row_count, both), F32),
            jax.ShapeDtypeStruct((seqs, 8, both), F32),
            jax.ShapeDtypeStruct((seqs, 8, wide), F32),
            jax.ShapeDtypeStruct((8, state), F32),
            jax.ShapeDtypeStruct((16, state), F32),
        ],
        in_specs=[smem] * 4 + [vmem] * 14,
        out_specs=[vmem] * 8,
        scratch_shapes=[
            VMEM((edge + row_count, wide), F32), VMEM((row_count + 8, wide), F32), VMEM((edge + row_count, both), F32),
            VMEM((seqs * row_count, both), F32), VMEM((seqs, 8, wide), F32), VMEM((groups - 1, rows, both), F32),
            VMEM(sums, F32), VMEM(sums, F32), VMEM((near,) + sums, F32), VMEM((chips // near,) + sums, F32),
            VMEM((groups, 16, state), F32),
        ]
        + [DMA((groups - 1,))] * 6
        + [DMA((1 + seqs,))] * 2
        + [DMA((near + chips // near + 1,))] * 2,
        compiler_params=pltpu.CompilerParams(collective_id=1, has_side_effects=True, vmem_limit_bytes=LIMIT),
    )(lengths, sb, dl, skip, feat, slope, kq, slope_bc, dt, cum, step, output_grad, inout, x_raw, px, bc_raw, pbc, wx)


def rows_kernel(
    size, dkq_ref, nsum_ref, bc_ref, pbc_ref, nbc_ref, wbc_ref, bbc_ref, nlead_ref, wx_ref, mixed_ref, gx_ref, dstep_ref,
    px_ref, pp_ref,
    mixed_out, gx_out, gbc_out, dstep_out, wx_out, bx_out, wbc_out, bbc_out, sb_out, dl_out, skip_out,
    ext_ref, dpre_ref, pad_ref,
):
    seqs, row_count, both = bc_ref.shape
    edge, taps, lead = pbc_ref.shape[1], wbc_ref.shape[0], nsum_ref.shape[1]
    state, wide, heads = both // 2, gx_ref.shape[2], dstep_ref.shape[1]
    inner = lax.axis_index("inner")
    has_before = jnp.where(inner > 0, 1.0, 0.0)
    has_after = jnp.where(inner < size - 1, 1.0, 0.0)
    start = edge - (taps - 1)
    wbc, wx = wbc_ref[...], wx_ref[...]
    mixed_out[...] = mixed_ref[...]
    dstep_out[...] = dstep_ref[...]
    for seq in range(seqs):
        ext_ref[:edge, :] = pbc_ref[seq].astype(F32) * has_before
        ext_ref[edge : edge + row_count, :] = bc_ref[seq].astype(F32)
        ext_ref[edge + row_count :, :] = nbc_ref[seq].astype(F32)
        pre = convolved(ext_ref, start, wbc, bbc_ref[...], row_count + lead)
        gate = sigmoid(pre)
        slope = gate * (1.0 + pre * (1.0 - gate))
        dpre_ref[:row_count, :] = dkq_ref[seq * row_count : (seq + 1) * row_count, :] * slope[:row_count, :]
        dpre_ref[row_count:, :] = nsum_ref[seq] * slope[row_count:, :] * has_after
        grad = jnp.zeros((row_count, both), F32)
        for tap in range(taps):
            shift = taps - 1 - tap
            grad = grad + wbc[tap : tap + 1] * dpre_ref[shift : shift + row_count, :]
        gbc_out[seq] = grad.astype(BF)

        pad_ref[:edge, :] = jnp.zeros((edge, wide), F32)
        pad_ref[edge : edge + lead, :] = nlead_ref[seq] * has_after
        gx_out[seq, : row_count - edge, :] = gx_ref[seq, : row_count - edge, :].astype(BF)
        tail = gx_ref[seq, row_count - edge :, :]
        for tap in range(taps):
            shift = taps - 1 - tap
            tail = tail + wx[tap : tap + 1] * pad_ref[shift : shift + edge, :]
        gx_out[seq, row_count - edge :, :] = tail.astype(BF)

    wx_out[...] = px_ref[:taps]
    bx_out[...] = px_ref[taps : taps + 1]
    for i, out in enumerate((sb_out, dl_out, skip_out)):
        out[...] = px_ref[taps + 1 + i : taps + 2 + i, :heads]
    wbc_out[:, :state] = pp_ref[:taps]
    wbc_out[:, state:] = pp_ref[8 : 8 + taps]
    bbc_out[:, :state] = pp_ref[taps : taps + 1]
    bbc_out[:, state:] = pp_ref[8 + taps : 9 + taps]


def bc_rows(dkq, nsum, bc_raw, pbc, nbc, wbc, bbc, nlead, wx, mixed, gx, dstep, px_sums, pbc_sums, size):
    seqs, row_count, both = bc_raw.shape
    edge, wide, lead, taps, heads = pbc.shape[1], gx.shape[2], nsum.shape[1], wx.shape[0], dstep.shape[1]
    vmem = pl.BlockSpec(memory_space=VMEM)
    shapes = (
        (mixed.shape, BF), (gx.shape, BF), (bc_raw.shape, BF), (dstep.shape, F32), ((taps, wide), F32), ((1, wide), F32),
        ((taps, both), F32), ((1, both), F32), ((1, heads), F32), ((1, heads), F32), ((1, heads), F32),
    )
    return pl.pallas_call(
        functools.partial(rows_kernel, size),
        name="rows",
        out_shape=[jax.ShapeDtypeStruct(*s) for s in shapes],
        in_specs=[vmem] * 14,
        out_specs=[vmem] * 11,
        scratch_shapes=[
            VMEM((edge + row_count + edge, both), F32), VMEM((row_count + lead, both), F32), VMEM((edge + lead, wide), F32)
        ],
        compiler_params=pltpu.CompilerParams(vmem_limit_bytes=LIMIT),
    )(dkq, nsum, bc_raw, pbc, nbc, wbc, bbc, nlead, wx, mixed, gx, dstep, px_sums, pbc_sums)


def per_device(
    sizes, x_raw, bc_raw, step_raw, lengths, conv_weight_x, conv_bias_x, conv_weight_bc, conv_bias_bc, step_bias,
    decay_log, skip_gain, output_grad,
):
    groups, size = sizes
    edge = 16
    bx, bbc = conv_bias_x[None], conv_bias_bc[None]
    step = jnp.swapaxes(step_raw, 1, 2)
    inout, feat, slope, kq, slope_bc, dt, cum, px, pbc, nbc = states(
        lengths, step_bias, decay_log, x_raw, bc_raw, step, output_grad, conv_weight_x, bx, conv_weight_bc, bbc, size, edge,
        32,
    )
    mixed, gx, dstep, dkq, nsum, nlead, px_sums, pbc_sums = back(
        lengths, step_bias, decay_log, skip_gain, feat, slope, kq, slope_bc, dt, cum, step, output_grad, inout, x_raw, px,
        bc_raw, pbc, conv_weight_x, groups, size,
    )
    mixed, gx, gbc, dstep, wx, bx_g, wbc, bbc_g, sb_g, dl_g, skip_g = bc_rows(
        dkq, nsum, bc_raw, pbc, nbc, conv_weight_bc, bbc, nlead, conv_weight_x, mixed, gx, dstep, px_sums, pbc_sums, size
    )
    return (mixed, gx, gbc, jnp.swapaxes(dstep, 1, 2), wx, bx_g[0], wbc, bbc_g[0], sb_g[0], dl_g[0], skip_g[0])


def solution(mesh):
    rows_and_heads = P(None, "inner", "outer")
    return jax.shard_map(
        functools.partial(per_device, (mesh.shape["outer"], mesh.shape["inner"])),
        mesh=mesh,
        in_specs=(
            rows_and_heads, P(None, "inner", None), rows_and_heads, P(), P(None, "outer"), P("outer"), P(), P(),
            P("outer"), P("outer"), P("outer"), rows_and_heads,
        ),
        out_specs=(
            rows_and_heads, rows_and_heads, P(None, "inner", None), rows_and_heads, P(None, "outer"), P("outer"), P(),
            P(), P("outer"), P("outer"), P("outer"),
        ),
        check_vma=False,
    )
```

```python
import functools
import types

import jax
import jax.numpy as jnp
from jax import lax
from jax.experimental import pallas as pl
from jax.experimental.pallas import tpu as pltpu
from jax.sharding import PartitionSpec as P

P_SIZE = 64
F32 = jnp.float32
BF = jnp.bfloat16
MESH = pl.DeviceIdType.MESH
VMEM = pltpu.VMEM
DMA = pltpu.SemaphoreType.DMA
LIMIT = 62 * 1024 * 1024
NN = ((1,), (0,))
NT = ((1,), (1,))
TN = ((0,), (0,))


def dot(a, b, dims):
    return lax.dot_general(a, b, (dims, ((), ())), preferred_element_type=F32)


def split(a):
    high = a.astype(BF)
    return high, (a - high.astype(F32)).astype(BF)


def split3(a):
    high = a.astype(BF)
    rest = a - high.astype(F32)
    mid = rest.astype(BF)
    return high, mid, (rest - mid.astype(F32)).astype(BF)


def mm(a, b, dims):
    out = dot(a[0], b[0], dims)
    if len(b) > 1:
        out = out + dot(a[0], b[1], dims)
    if len(a) > 1:
        out = out + dot(a[1], b[0], dims)
    return out


def mm_exact(parts, ones, dims):
    out = dot(parts[0], ones, dims)
    for part in parts[1:]:
        out = out + dot(part, ones, dims)
    return out


def mm_exact_left(ones, parts, dims):
    out = dot(ones, parts[0], dims)
    for part in parts[1:]:
        out = out + dot(ones, part, dims)
    return out


def iota(shape, dim):
    return lax.broadcasted_iota(jnp.int32, shape, dim)


def head_ones(heads, width):
    row, col = iota((heads, width), 0), iota((heads, width), 1)
    return jnp.where((col >= row * P_SIZE) & (col < (row + 1) * P_SIZE), 1.0, 0.0).astype(BF)


def spread(per_head, ones):
    return mm_exact(split3(per_head), ones, TN)


def head_sums(a, ones):
    return mm_exact_left(ones, split3(a), NT)


def columns(per_head, eye):
    return mm_exact_left(eye, split3(per_head), NT)


def to_row(column):
    heads = column.shape[0]
    same = iota((heads, heads), 0) == iota((heads, heads), 1)
    return jnp.sum(jnp.where(same, column, 0.0), axis=0, keepdims=True)


def scalars(ref, shape, dim, each):
    place = iota(shape, dim)
    out = jnp.full(shape, ref[0], F32)
    for i in range(1, ref.shape[0]):
        out = jnp.where(place >= i * each, ref[i], out)
    return out


def triangle(rows, upper):
    row, col = iota((rows, rows), 0), iota((rows, rows), 1)
    return jnp.where(col >= row if upper else row >= col, 1.0, 0.0).astype(BF)


def convolved(ext_ref, start, weight, bias, row_count):
    pre_act = bias
    for tap in range(weight.shape[0]):
        pre_act = pre_act + weight[tap : tap + 1] * ext_ref[start + tap : start + tap + row_count, :]
    return pre_act


def softplus(z):
    return jnp.maximum(z, 0.0) + jnp.log1p(jnp.exp(-jnp.abs(z)))


def sigmoid(z):
    return 1.0 / (1.0 + jnp.exp(-z))


def valid_rows(lengths_ref, seq, row_count, dim):
    first = lax.axis_index("inner") * row_count
    shape = (row_count, 1) if dim == 0 else (1, row_count)
    return jnp.where(first + iota(shape, dim) < lengths_ref[seq], 1.0, 0.0)


def remote(src, dst, send, recv, **where):
    return pltpu.make_async_remote_copy(
        src_ref=src, dst_ref=dst, send_sem=send, recv_sem=recv, device_id=where, device_id_type=MESH
    )


def greet(**where):
    pl.semaphore_signal(pltpu.get_barrier_semaphore(), inc=1, device_id=where, device_id_type=MESH)


def loop(first, count, do):
    def body(i, carry):
        do(i)
        return carry

    lax.fori_loop(first, count, body, 0)


INS = (
    "lengths_in", "sb_in", "dl_in", "skip_in", "x_in", "bc_in", "step_in", "og_in", "wx_in", "bx_in", "wbc_in", "bbc_in",
)
OUTS = (
    "mixed_out", "gx_out", "gbc_out", "dstep_out", "wx_out", "bx_out", "wbc_out", "bbc_out", "sb_out", "dl_out", "skip_out",
)
DIRECT = 4


def layout(seqs, row_count, wide, both, heads, taps, edge, groups, chips, near, pieces):
    state, rows = both // 2, seqs * row_count // groups
    blocks, flat = chips // near, (seqs * wide, state)
    smem, i32 = pltpu.SMEM, jnp.int32
    return {
        "lengths": smem((seqs,), i32), "sb": smem((heads,), F32), "dl": smem((heads,), F32), "skip": smem((heads,), F32),
        "x": VMEM((seqs, row_count, wide), BF), "bc": VMEM((seqs, row_count, both), BF),
        "step": VMEM((seqs, heads, row_count), F32), "og": VMEM((seqs, row_count, wide), BF),
        "wx": VMEM((taps, wide), F32), "bx": VMEM((1, wide), F32), "wbc": VMEM((taps, both), F32),
        "bbc": VMEM((1, both), F32), "load": DMA((len(INS),)),
        "px": VMEM((seqs, edge, wide), BF), "pbc": VMEM((seqs, edge, both), BF), "nbc": VMEM((seqs, edge, both), BF),
        "mixed": VMEM((seqs, row_count, wide), BF), "gx": VMEM((seqs, row_count, wide), BF),
        "gx_tail": VMEM((seqs, edge, wide), F32), "gbc": VMEM((seqs, row_count, both), BF),
        "dstep": VMEM((seqs, heads, row_count), F32), "store": DMA((DIRECT,)),
        "extx": VMEM((seqs, edge + row_count, wide), F32), "extbc": VMEM((seqs, 2 * edge + row_count, both), F32),
        "feat": VMEM((seqs, row_count, wide), F32), "slope": VMEM((seqs, row_count, wide), F32),
        "kq": VMEM((seqs, row_count, both), F32), "slope_bc": VMEM((seqs, row_count, both), F32),
        "weight": VMEM((seqs, row_count, wide), F32), "grown": VMEM((seqs, row_count, wide), F32),
        "dt": VMEM((seqs, heads, row_count), F32), "cum": VMEM((seqs, heads, row_count), F32),
        "within": VMEM((seqs, row_count, wide), F32), "dfeat": VMEM((seqs, row_count, wide), F32),
        "dscores": VMEM((seqs, row_count, row_count), F32),
        "row_part": VMEM((seqs, heads, row_count), F32), "col_part": VMEM((seqs, heads, row_count), F32),
        "dpre": VMEM((row_count + 8, wide), F32), "lead": VMEM((seqs, 8, wide), F32),
        "dkq": VMEM((seqs * row_count, both), F32), "total": VMEM((seqs * row_count, both), F32),
        "next_total": VMEM((seqs, 8, both), F32), "next_lead": VMEM((seqs, 8, wide), F32),
        "dpre_bc": VMEM((row_count + 8, both), F32), "pad": VMEM((edge + 8, wide), F32),
        "edge_send": DMA((4,)), "edge_recv": DMA((4,)),
        "own": VMEM((2,) + flat, F32), "other": VMEM(flat, F32), "io": VMEM((2,) + flat, F32), "after": VMEM(flat, F32),
        "decay": VMEM((seqs, heads, state), F32), "odecay": VMEM((seqs, heads, state), F32),
        "joined": VMEM(flat, F32), "both": VMEM((seqs, heads, state), F32),
        "later": VMEM(flat, F32), "later_in": VMEM(flat, F32), "shrink": VMEM((seqs, heads, state), F32),
        "shrink_in": VMEM((seqs, heads, state), F32), "ahead": VMEM(flat, F32), "beyond": VMEM(flat, F32),
        "swap_send": DMA((pieces,)), "swap_recv": DMA((pieces,)), "hand_send": DMA((pieces,)), "hand_recv": DMA((pieces,)),
        "later_send": DMA((pieces + 1,)), "later_recv": DMA((pieces + 1,)),
        "step_send": DMA((pieces,)), "skip_send": DMA((pieces,)), "chain_recv": DMA((pieces,)),
        "slots": VMEM((groups - 1, rows, both), F32),
        "scatter_send": DMA((groups,)), "scatter_recv": DMA((groups,)),
        "gather_send": DMA((groups,)), "gather_recv": DMA((groups,)),
        "rim_send": DMA((groups,)), "rim_recv": DMA((seqs + 1,)), "lead_send": DMA((1,)),
        "outer": VMEM((groups, 16, state), F32), "outer_send": DMA((groups,)), "outer_recv": DMA((groups,)),
        "x_mine": VMEM((8, wide), F32), "x_mate": VMEM((8, wide), F32), "x_near": VMEM((near, 8, wide), F32),
        "x_far": VMEM((blocks, 8, wide), F32), "x_send": DMA((near + blocks,)), "x_recv": DMA((near + blocks,)),
        "p_mine": VMEM((16, state), F32), "p_mate": VMEM((16, state), F32), "p_near": VMEM((near, 16, state), F32),
        "p_far": VMEM((blocks, 16, state), F32), "p_send": DMA((near + blocks,)), "p_recv": DMA((near + blocks,)),
    }


def activate(r, seq, first, rows):
    edge, taps = r.px.shape[1], r.wx.shape[0]
    where = pl.ds(first, rows)
    for ext, weight, bias, value, slope in (
        (r.extx, r.wx, r.bx, r.feat, r.slope),
        (r.extbc, r.wbc, r.bbc, r.kq, r.slope_bc),
    ):
        pre = convolved(ext.at[seq], edge - (taps - 1) + first, weight[...], bias[...], rows)
        gate = sigmoid(pre)
        value[seq, where, :] = pre * gate
        slope[seq, where, :] = gate * (1.0 + pre * (1.0 - gate))


def local_states(r, seq):
    state = r.kq.shape[2] // 2
    dy = r.og[seq].astype(F32)
    keys, queries = split(r.kq[seq, :, :state]), split(r.kq[seq, :, state:])
    return (
        mm(split(r.weight[seq] * r.feat[seq]), keys, TN),
        mm(split(r.grown[seq] * dy), queries, TN),
    )


def inside(r, seq):
    row_count, wide = r.feat.shape[1:]
    heads, state = r.dt.shape[1], r.kq.shape[2] // 2
    dy = r.og[seq].astype(F32) * valid_rows(r.lengths, seq, row_count, 0)
    dy_b = dy.astype(BF)
    feats, keys, queries = split(r.feat[seq]), split(r.kq[seq, :, :state]), split(r.kq[seq, :, state:])
    lane = iota((1, wide), 1)
    row, col = iota((row_count, row_count), 0), iota((row_count, row_count), 1)
    causal = row >= col
    eye = jnp.where(row == col, 1.0, 0.0).astype(BF)
    dt, cum = r.dt[seq], r.cum[seq]
    cum_cols = columns(cum, eye)
    scores = mm(queries, keys, NT)
    within = jnp.zeros((row_count, wide), F32)
    dfeat = jnp.zeros((row_count, wide), F32)
    dscores = jnp.zeros((row_count, row_count), F32)
    row_sums, col_sums = [], []
    for head in range(heads):
        gap = cum_cols[:, head : head + 1] - cum[head : head + 1, :]
        decays = jnp.where(causal, jnp.exp(jnp.where(causal, gap, 0.0)), 0.0)
        stepped = decays * dt[head : head + 1, :]
        mixing = stepped * scores
        here = (lane >= head * P_SIZE) & (lane < (head + 1) * P_SIZE)
        within = jnp.where(here, mm(split(mixing), feats, NN), within)
        dfeat = jnp.where(here, mm(split(mixing.T), (dy_b,), NN), dfeat)
        dmixing = mm((jnp.where(here, dy, 0.0).astype(BF),), feats, NT)
        dscores = dscores + dmixing * stepped
        row_sums.append(jnp.sum(dmixing * mixing, axis=1, keepdims=True))
        col_sums.append(jnp.sum(dmixing * decays * scores, axis=0, keepdims=True))
    r.within[seq] = within
    r.dfeat[seq] = dfeat
    r.dscores[seq] = dscores
    r.row_part[seq] = mm_exact(split3(jnp.concatenate(row_sums, axis=1)), eye, TN)
    r.col_part[seq] = jnp.concatenate(col_sums, axis=0)


def rows_back(r, seq):
    row_count, wide = r.feat.shape[1:]
    state = r.kq.shape[2] // 2
    block, rows = pl.ds(seq * wide, wide), pl.ds(seq * row_count, row_count)
    dy = r.og[seq].astype(F32) * valid_rows(r.lengths, seq, row_count, 0)
    keys, queries = split(r.kq[seq, :, :state]), split(r.kq[seq, :, state:])
    dscores = r.dscores[seq]
    r.dkq[rows, state:] = mm(split(dscores), keys, NN) + mm(split(r.grown[seq] * dy), split(r.io[0, block, :]), NN)
    r.dkq[rows, :state] = mm(split(dscores.T), queries, NN) + mm(
        split(r.weight[seq] * r.feat[seq]), split(r.io[1, block, :]), NN
    )


def heads_back(r, seq):
    row_count, wide = r.feat.shape[1:]
    edge, taps, heads, state = r.px.shape[1], r.wx.shape[0], r.dt.shape[1], r.kq.shape[2] // 2
    block = pl.ds(seq * wide, wide)
    valid = valid_rows(r.lengths, seq, row_count, 0)
    dy = r.og[seq].astype(F32) * valid
    feat, dt, cum = r.feat[seq], r.dt[seq], r.cum[seq]
    incoming, later = r.io[0, block, :], r.io[1, block, :]
    ones = head_ones(heads, wide)
    skip = scalars(r.skip, (1, wide), 1, P_SIZE)
    carried = mm(split(r.kq[seq, :, state:]), split(incoming), NT) * r.grown[seq]
    r.mixed[seq] = ((r.within[seq] + carried + skip * feat) * valid).astype(BF)
    back = mm(split(r.kq[seq, :, :state]), split(later), NT)
    dfeat = r.dfeat[seq] + skip * dy + r.weight[seq] * back

    total = cum[:, row_count - 1 :]
    col_part = r.col_part[seq]
    back_left = head_sums(feat * back, ones) * jnp.exp(total - cum)
    dcum = r.row_part[seq] + head_sums(dy * carried, ones) - (col_part + back_left) * dt
    later_in = jnp.sum(mm_exact_left(ones, split3(later * incoming), NN), axis=1, keepdims=True)
    dtotal = jnp.sum(back_left * dt, axis=1, keepdims=True) + later_in * jnp.exp(total)
    drun = mm_exact(split3(dcum), triangle(row_count, False), NN) + dtotal
    rate = -jnp.exp(scalars(r.dl, (heads, 1), 0, 1))
    z = r.step[seq] + scalars(r.sb, (heads, 1), 0, 1)
    dstep = (col_part + back_left + drun * rate) * valid_rows(r.lengths, seq, row_count, 1) * sigmoid(z)
    r.dstep[seq] = dstep
    ddecay = jnp.sum(drun * dt, axis=1, keepdims=True) * rate
    dskip = jnp.sum(head_sums(dy * feat, ones), axis=1, keepdims=True)

    dpre = dfeat * r.slope[seq]
    r.lead[seq] = dpre[:8, :]
    r.dpre[:row_count, :] = dpre
    r.dpre[row_count:, :] = jnp.zeros((8, wide), F32)
    gx = jnp.zeros((row_count, wide), F32)
    for tap in range(taps):
        shift = taps - 1 - tap
        gx = gx + r.wx[tap : tap + 1, :] * r.dpre[shift : shift + row_count, :]
    r.gx[seq] = gx.astype(BF)
    r.gx_tail[seq] = gx[row_count - edge :, :]
    start = edge - (taps - 1)
    for tap in range(taps):
        term = dpre * r.extx[seq, start + tap : start + tap + row_count, :]
        r.x_mine[tap : tap + 1, :] += jnp.sum(term, axis=0, keepdims=True)
    r.x_mine[taps : taps + 1, :] += jnp.sum(dpre, axis=0, keepdims=True)
    for i, part in enumerate((jnp.sum(dstep, axis=1, keepdims=True), ddecay, dskip)):
        r.x_mine[taps + 1 + i : taps + 2 + i, :heads] += to_row(part)


def last_rows(r, seq, has_after):
    edge, taps, row_count = r.px.shape[1], r.wx.shape[0], r.x.shape[1]
    lead, wide = r.next_lead.shape[1:]
    r.pad[:edge, :] = jnp.zeros((edge, wide), F32)
    r.pad[edge:, :] = r.next_lead[seq] * has_after
    tail = r.gx_tail[seq]
    for tap in range(taps):
        shift = taps - 1 - tap
        tail = tail + r.wx[tap : tap + 1, :] * r.pad[shift : shift + edge, :]
    r.gx[seq, row_count - edge :, :] = tail.astype(BF)


def bc_grads(r, seq, has_after):
    edge, taps, row_count = r.px.shape[1], r.wx.shape[0], r.x.shape[1]
    lead, both = r.next_total.shape[1:]
    pre = convolved(r.extbc.at[seq], edge - (taps - 1) + row_count, r.wbc[...], r.bbc[...], lead)
    gate = sigmoid(pre)
    slope = gate * (1.0 + pre * (1.0 - gate))
    r.dpre_bc[:row_count, :] = r.total[seq * row_count : (seq + 1) * row_count, :] * r.slope_bc[seq]
    r.dpre_bc[row_count:, :] = r.next_total[seq] * slope * has_after
    grad = jnp.zeros((row_count, both), F32)
    for tap in range(taps):
        shift = taps - 1 - tap
        grad = grad + r.wbc[tap : tap + 1, :] * r.dpre_bc[shift : shift + row_count, :]
    r.gbc[seq] = grad.astype(BF)


def far_place(chips, core, place):
    return jnp.where(core == 0, place, chips - 1 - place) * 2 + core


def mixer_kernel(names, groups, size, near, pieces, *refs):
    r = types.SimpleNamespace(**dict(zip(names, refs)))
    seqs, row_count, wide = r.x.shape
    both, heads, edge, taps = r.bc.shape[2], r.dt.shape[1], r.px.shape[1], r.wx.shape[0]
    state, chips = both // 2, size // 2
    blocks = chips // near
    me, inner = lax.axis_index("outer"), lax.axis_index("inner")
    after, before = lax.rem(inner + 1, size), lax.rem(inner + size - 1, size)
    chip, core = inner // 2, lax.rem(inner, 2)
    mate = chip * 2 + 1 - core
    chip_block, chip_spot = chip // near, lax.rem(chip, near)
    shares = groups // seqs
    owner = lax.rem(me, shares) == 0

    def near_peer(d):
        return (chip_block * near + lax.rem(chip_spot + d, near)) * 2 + core

    def far_peer(d):
        return (lax.rem(chip_block + d, blocks) * near + chip_spot) * 2 + core

    def around(d):
        return lax.rem(me + d, groups)

    ahead = lax.rem(chip + 1 - 2 * core + chips, chips) * 2 + core
    behind = lax.rem(chip - 1 + 2 * core + chips, chips) * 2 + core
    loads = {
        name: pltpu.make_async_copy(getattr(r, name), getattr(r, name[:-3]), r.load.at[i]) for i, name in enumerate(INS)
    }
    for copy in loads.values():
        copy.start()
    peers = [after, before, mate, ahead, behind]
    peers += [near_peer(d) for d in range(1, near)] + [far_peer(d) for d in range(1, blocks)]
    for other in peers:
        greet(inner=other)
    loop(1, groups, lambda d: greet(outer=around(d)))
    for seq in range(seqs):
        greet(outer=seq * shares, inner=after)
    for name in ("lengths_in", "sb_in", "dl_in", "step_in"):
        loads[name].wait()

    ones = head_ones(heads, wide)
    rate = -jnp.exp(scalars(r.dl, (heads, 1), 0, 1))
    bias = scalars(r.sb, (heads, 1), 0, 1)
    for seq in range(seqs):
        dt = softplus(r.step[seq] + bias) * valid_rows(r.lengths, seq, row_count, 1)
        cum = mm_exact(split3(dt * rate), triangle(row_count, True), NN)
        r.dt[seq] = dt
        r.cum[seq] = cum
        r.decay[seq] = jnp.broadcast_to(jnp.exp(cum[:, row_count - 1 :]), (heads, state))
        r.weight[seq] = spread(jnp.exp(cum[:, row_count - 1 :] - cum) * dt, ones)
        r.grown[seq] = spread(jnp.exp(cum), ones) * valid_rows(r.lengths, seq, row_count, 0)
    r.x_mine[...] = jnp.zeros(r.x_mine.shape, F32)
    r.p_mine[...] = jnp.zeros(r.p_mine.shape, F32)
    for name in INS:
        if name not in ("lengths_in", "sb_in", "dl_in", "step_in"):
            loads[name].wait()

    def begin(seq):
        r.extx[seq, edge:, :] = r.x[seq].astype(F32)
        r.extbc[seq, edge : edge + row_count, :] = r.bc[seq].astype(F32)
        activate(r, seq, edge, row_count - edge)

    begin(0)
    pl.semaphore_wait(
        pltpu.get_barrier_semaphore(), len(peers) + groups - 1 + jnp.where(owner, groups, 0)
    )

    tail = pl.ds(row_count - edge, edge)
    rims = [
        remote(r.bc.at[:, tail, :], r.pbc, r.edge_send.at[1], r.edge_recv.at[1], inner=after),
        remote(r.x.at[:, tail, :], r.px, r.edge_send.at[0], r.edge_recv.at[0], inner=after),
        remote(r.bc.at[:, pl.ds(0, edge), :], r.nbc, r.edge_send.at[2], r.edge_recv.at[2], inner=before),
    ]
    for copy in rims:
        copy.start()
    decays = remote(r.decay, r.odecay, r.edge_send.at[3], r.edge_recv.at[3], inner=mate)
    decays.start()
    for seq in range(1, seqs):
        begin(seq)

    rows = seqs * wide // pieces
    per_head, per_seq = P_SIZE // rows, wide // rows

    def piece(j):
        return pl.ds(pl.multiple_of(j * rows, rows), rows)

    def swap(j):
        return remote(
            r.own.at[1 - core, piece(j), :], r.other.at[piece(j), :], r.swap_send.at[j], r.swap_recv.at[j], inner=mate
        )

    keep = jnp.where(inner > 0, 1.0, 0.0)
    rims[0].wait_recv()
    rims[1].wait_recv()
    for seq in range(seqs):
        r.extx[seq, :edge, :] = r.px[seq].astype(F32) * keep
        r.extbc[seq, :edge, :] = r.pbc[seq].astype(F32) * keep
        activate(r, seq, 0, edge)
        for kind, value in enumerate(local_states(r, seq)):
            r.own[kind, seq * wide : (seq + 1) * wide, :] = value
        loop(seq * per_seq, (seq + 1) * per_seq, lambda j: swap(j).start())

    place = jnp.where(core == 0, chip, chips - 1 - chip)
    block, spot = place // near, lax.rem(place, near)
    opens, ends = place == 0, spot == near - 1
    summed = (block > 0) & (block < blocks - 1)
    skips = summed & (spot == 0)
    steps = jnp.logical_not(ends) | (block == 0)
    busy_first = (block < blocks - 2) | ((block == blocks - 2) & (spot == 0))
    further = far_place(chips, core, place + near)

    def seq_head(j):
        head = j // per_head
        return head // heads, pl.ds(lax.rem(head, heads), 1)

    def send_later(j):
        return remote(
            r.later.at[piece(j), :], r.later_in.at[piece(j), :], r.later_send.at[j], r.later_recv.at[j], inner=behind
        )

    def send_shrink():
        return remote(r.shrink, r.shrink_in, r.later_send.at[pieces], r.later_recv.at[pieces], inner=behind)

    def step(j):
        return remote(
            r.ahead.at[piece(j), :], r.io.at[core, piece(j), :], r.step_send.at[j], r.chain_recv.at[j], inner=ahead
        )

    def skip(j):
        return remote(
            r.beyond.at[piece(j), :], r.io.at[core, piece(j), :], r.skip_send.at[j], r.chain_recv.at[j], inner=further
        )

    def hand(j, kind):
        return remote(
            r.after.at[piece(j), :], r.io.at[kind, piece(j), :], r.hand_send.at[j], r.hand_recv.at[j], inner=mate
        )

    decays.wait_recv()
    r.both[...] = r.decay[...] * r.odecay[...]

    @pl.when(summed & ends)
    def _():
        r.shrink[...] = r.both[...]
        send_shrink().start()

    @pl.when(opens)
    def _():
        r.io[core] = jnp.zeros((seqs * wide, state), F32)

    def join(j):
        swap(j).wait_recv()
        seq, head = seq_head(j)
        joined = r.odecay[seq, head, :] * r.own[core, piece(j), :] + r.other[piece(j), :]
        r.joined[piece(j), :] = joined

        @pl.when(summed & ends)
        def _():
            r.later[piece(j), :] = joined
            send_later(j).start()

        @pl.when(opens)
        def _():
            r.ahead[piece(j), :] = joined
            step(j).start()

    loop(0, pieces, join)

    @pl.when(summed & jnp.logical_not(ends))
    def _():
        send_shrink().wait_recv()
        r.shrink[...] = r.both[...] * r.shrink_in[...]

        @pl.when(spot > 0)
        def _():
            send_shrink().start()

        def sum_up(j):
            seq, head = seq_head(j)
            send_later(j).wait_recv()
            r.later[piece(j), :] = r.shrink_in[seq, head, :] * r.joined[piece(j), :] + r.later_in[piece(j), :]

            @pl.when(spot > 0)
            def _():
                send_later(j).start()

        loop(0, pieces, sum_up)

    @pl.when(jnp.logical_not(busy_first))
    def _():
        loop(0, seqs, lambda seq: inside(r, seq))

    def go_on(j):
        seq, head = seq_head(j)
        r.ahead[piece(j), :] = r.both[seq, head, :] * r.io[core, piece(j), :] + r.joined[piece(j), :]
        step(j).start()

    def pass_on(j):
        seq, head = seq_head(j)

        @pl.when(jnp.logical_not(opens))
        def _():
            step(j).wait_recv()

        @pl.when(skips)
        def _():
            r.beyond[piece(j), :] = r.shrink[seq, head, :] * r.io[core, piece(j), :] + r.later[piece(j), :]
            skip(j).start()

        @pl.when(steps & jnp.logical_not(skips | opens))
        def _():
            go_on(j)

        r.after[piece(j), :] = r.decay[seq, head, :] * r.io[core, piece(j), :] + r.own[core, piece(j), :]
        hand(j, core).start()

    loop(0, pieces, pass_on)

    @pl.when(skips)
    def _():
        loop(0, pieces, go_on)

    @pl.when(busy_first)
    def _():
        loop(0, seqs, lambda seq: inside(r, seq))

    loop(0, pieces, lambda j: hand(j, 1 - core).wait_recv())

    share_rows = seqs * row_count // groups

    def share_of(index):
        return pl.ds(pl.multiple_of(index * share_rows, share_rows), share_rows)

    def scatter(d):
        to = around(d)
        return remote(
            r.dkq.at[share_of(to), :], r.slots.at[d - 1], r.scatter_send.at[d], r.scatter_recv.at[d], outer=to
        )

    def gather(d, source):
        part = r.total.at[share_of(source), :]
        return remote(part, part, r.gather_send.at[d], r.gather_recv.at[d], outer=around(d))

    def gather_params(d, source):
        part = r.outer.at[source]
        return remote(part, part, r.outer_send.at[d], r.outer_recv.at[d], outer=around(d))

    lead = r.next_total.shape[1]

    def rim(to, seq):
        return remote(
            r.total.at[pl.ds(seq * row_count, lead), :], r.next_total.at[seq], r.rim_send.at[to], r.rim_recv.at[seq],
            outer=to, inner=before,
        )

    def source(d):
        return lax.rem(me + groups - d, groups)

    leaves = []

    def stage(buf, index, many, peer, send, recv, first):
        for d in range(1, many):
            remote(buf.at[index], buf.at[index], send.at[first + d], recv.at[first + d], inner=peer(d)).start()

        def finish():
            for d in range(1, many):
                part = buf.at[lax.rem(index + many - d, many)]
                remote(part, part, send.at[first + d], recv.at[first + d], inner=peer(d)).wait_recv()
            total = buf[0]
            for k in range(1, many):
                total = total + buf[k]
            return total

        def leave():
            for d in range(1, many):
                part = buf.at[index]
                remote(part, part, send.at[first + d], recv.at[first + d], inner=peer(d)).wait_send()

        leaves.append(leave)
        return finish

    for seq in range(seqs):
        rows_back(r, seq)

    loop(1, groups, lambda d: scatter(d).start())

    start = edge - (taps - 1)
    for seq in range(seqs):
        dpre = r.dkq[seq * row_count : (seq + 1) * row_count, :] * r.slope_bc[seq]
        for tap in range(taps + 1):
            term = dpre if tap == taps else dpre * r.extbc[seq, start + tap : start + tap + row_count, :]
            term = jnp.sum(term, axis=0, keepdims=True)
            r.p_mine[tap : tap + 1, :] += term[:, :state]
            r.p_mine[8 + tap : 9 + tap, :] += term[:, state:]
    p_mate = remote(r.p_mine, r.p_mate, r.p_send.at[0], r.p_recv.at[0], inner=mate)
    p_mate.start()
    p_mate.wait()
    r.p_near[chip_spot] = r.p_mine[...] + r.p_mate[...]
    p_finish = stage(r.p_near, chip_spot, near, near_peer, r.p_send, r.p_recv, 0)
    for seq in range(seqs):
        heads_back(r, seq)
    x_mate = remote(r.x_mine, r.x_mate, r.x_send.at[0], r.x_recv.at[0], inner=mate)
    x_mate.start()
    leads = remote(r.lead, r.next_lead, r.lead_send.at[0], r.rim_recv.at[seqs], inner=before)
    leads.start()
    stores = [
        pltpu.make_async_copy(getattr(r, name[:-4]), getattr(r, name), r.store.at[i])
        for i, name in enumerate(OUTS[:DIRECT])
    ]
    stores[0].start()
    stores[3].start()
    r.p_far[chip_block] = p_finish()
    p_finish = stage(r.p_far, chip_block, blocks, far_peer, r.p_send, r.p_recv, near)
    x_mate.wait()
    r.x_near[chip_spot] = r.x_mine[...] + r.x_mate[...]
    x_finish = stage(r.x_near, chip_spot, near, near_peer, r.x_send, r.x_recv, 0)

    loop(1, groups, lambda d: scatter(d).wait_recv())
    acc = r.dkq[share_of(me), :]
    for d in range(groups - 1):
        acc = acc + r.slots[d]
    r.total[share_of(me), :] = acc
    loop(1, groups, lambda d: gather(d, me).start())

    @pl.when(owner)
    def _():
        loop(0, groups, lambda to: rim(to, me // shares).start())

    r.x_far[chip_block] = x_finish()
    x_finish = stage(r.x_far, chip_block, blocks, far_peer, r.x_send, r.x_recv, near)
    r.outer[me] = p_finish()
    loop(1, groups, lambda d: gather_params(d, me).start())
    loop(1, groups, lambda d: gather(d, source(d)).wait_recv())
    for seq in range(seqs):
        rim(me, seq).wait_recv()
    has_after = jnp.where(inner < size - 1, 1.0, 0.0)
    rims[2].wait_recv()
    leads.wait_recv()
    for seq in range(seqs):
        r.extbc[seq, edge + row_count :, :] = r.nbc[seq].astype(F32)
        last_rows(r, seq, has_after)
        bc_grads(r, seq, has_after)
    stores[1].start()
    stores[2].start()
    total = x_finish()
    r.wx_out[...] = total[:taps]
    r.bx_out[...] = total[taps : taps + 1]
    for i, out in enumerate((r.sb_out, r.dl_out, r.skip_out)):
        out[...] = total[taps + 1 + i : taps + 2 + i, :heads]

    for leave in leaves:
        leave()
    for copy in rims:
        copy.wait_send()
    decays.wait_send()
    leads.wait_send()

    def sent(j):
        swap(j).wait_send()
        hand(j, core).wait_send()

        @pl.when(summed & (spot > 0))
        def _():
            send_later(j).wait_send()

        @pl.when(steps)
        def _():
            step(j).wait_send()

        @pl.when(skips)
        def _():
            skip(j).wait_send()

    loop(0, pieces, sent)

    @pl.when(summed & (spot > 0))
    def _():
        send_shrink().wait_send()

    @pl.when(owner)
    def _():
        loop(0, groups, lambda to: rim(to, me // shares).wait_send())

    def gone(d):
        scatter(d).wait_send()
        gather(d, me).wait_send()

    loop(1, groups, gone)
    for copy in stores:
        copy.wait()
    loop(1, groups, lambda d: gather_params(d, source(d)).wait_recv())
    total = r.outer[0]
    for k in range(1, groups):
        total = total + r.outer[k]
    r.wbc_out[:, :state] = total[:taps]
    r.wbc_out[:, state:] = total[8 : 8 + taps]
    r.bbc_out[:, :state] = total[taps : taps + 1]
    r.bbc_out[:, state:] = total[8 + taps : 9 + taps]

    def drain(d):
        gather_params(d, me).wait_send()

    loop(1, groups, drain)


def mixer(lengths, sb, dl, skip, x_raw, bc_raw, step, output_grad, wx, bx, wbc, bbc, groups, size, edge):
    seqs, row_count, wide = x_raw.shape
    both, heads, taps = bc_raw.shape[2], step.shape[1], wx.shape[0]
    state, chips = both // 2, size // 2
    near = 4 if chips % 4 == 0 else 1
    pieces = 16
    scratch = layout(seqs, row_count, wide, both, heads, taps, edge, groups, chips, near, pieces)
    shapes = (
        ((seqs, row_count, wide), BF), ((seqs, row_count, wide), BF), ((seqs, row_count, both), BF),
        ((seqs, heads, row_count), F32), ((taps, wide), F32), ((1, wide), F32), ((taps, both), F32), ((1, both), F32),
        ((1, heads), F32), ((1, heads), F32), ((1, heads), F32),
    )
    return pl.pallas_call(
        functools.partial(mixer_kernel, INS + OUTS + tuple(scratch), groups, size, near, pieces),
        name="mixer",
        out_shape=[jax.ShapeDtypeStruct(*s) for s in shapes],
        in_specs=[pl.BlockSpec(memory_space=pltpu.HBM)] * len(INS),
        out_specs=[pl.BlockSpec(memory_space=pltpu.HBM)] * DIRECT + [pl.BlockSpec(memory_space=VMEM)] * (len(OUTS) - DIRECT),
        scratch_shapes=list(scratch.values()),
        compiler_params=pltpu.CompilerParams(collective_id=0, has_side_effects=True, vmem_limit_bytes=LIMIT),
    )(lengths, sb, dl, skip, x_raw, bc_raw, step, output_grad, wx, bx, wbc, bbc)


def hand_on_kernel(*refs):
    count = len(OUTS)
    for taken, given in zip(refs[:count], refs[count:]):
        given[...] = taken[...]


def hand_on(arrays):
    specs = [pl.BlockSpec(memory_space=VMEM)] * len(arrays)
    return pl.pallas_call(
        hand_on_kernel,
        name="hand_on",
        out_shape=[jax.ShapeDtypeStruct(a.shape, a.dtype) for a in arrays],
        in_specs=specs,
        out_specs=specs,
        compiler_params=pltpu.CompilerParams(vmem_limit_bytes=LIMIT),
    )(*arrays)


def per_device(
    sizes, x_raw, bc_raw, step_raw, lengths, conv_weight_x, conv_bias_x, conv_weight_bc, conv_bias_bc, step_bias,
    decay_log, skip_gain, output_grad,
):
    groups, size = sizes
    edge = 16
    bx, bbc = conv_bias_x[None], conv_bias_bc[None]
    step = jnp.swapaxes(step_raw, 1, 2)
    mixed, gx, gbc, dstep, wx, bx_g, wbc, bbc_g, sb_g, dl_g, skip_g = hand_on(
        mixer(
            lengths, step_bias, decay_log, skip_gain, x_raw, bc_raw, step, output_grad, conv_weight_x, bx, conv_weight_bc,
            bbc, groups, size, edge,
        )
    )
    return (mixed, gx, gbc, jnp.swapaxes(dstep, 1, 2), wx, bx_g[0], wbc, bbc_g[0], sb_g[0], dl_g[0], skip_g[0])


def solution(mesh):
    rows_and_heads = P(None, "inner", "outer")
    return jax.shard_map(
        functools.partial(per_device, (mesh.shape["outer"], mesh.shape["inner"])),
        mesh=mesh,
        in_specs=(
            rows_and_heads, P(None, "inner", None), rows_and_heads, P(), P(None, "outer"), P("outer"), P(), P(),
            P("outer"), P("outer"), P("outer"), rows_and_heads,
        ),
        out_specs=(
            rows_and_heads, rows_and_heads, P(None, "inner", None), rows_and_heads, P(None, "outer"), P("outer"), P(),
            P(), P("outer"), P("outer"), P("outer"),
        ),
        check_vma=False,
    )
```

```python
import functools
import types

import jax
import jax.numpy as jnp
from jax import lax
from jax.experimental import pallas as pl
from jax.experimental.pallas import tpu as pltpu
from jax.sharding import PartitionSpec as P

P_SIZE = 64
F32 = jnp.float32
BF = jnp.bfloat16
MESH = pl.DeviceIdType.MESH
VMEM = pltpu.VMEM
DMA = pltpu.SemaphoreType.DMA
LIMIT = 62 * 1024 * 1024
NN = ((1,), (0,))
NT = ((1,), (1,))
TN = ((0,), (0,))


def dot(a, b, dims):
    return lax.dot_general(a, b, (dims, ((), ())), preferred_element_type=F32)


def split(a):
    high = a.astype(BF)
    return high, (a - high.astype(F32)).astype(BF)


def split3(a):
    high = a.astype(BF)
    rest = a - high.astype(F32)
    mid = rest.astype(BF)
    return high, mid, (rest - mid.astype(F32)).astype(BF)


def mm(a, b, dims):
    out = dot(a[0], b[0], dims)
    if len(b) > 1:
        out = out + dot(a[0], b[1], dims)
    if len(a) > 1:
        out = out + dot(a[1], b[0], dims)
    return out


def mm_exact(parts, ones, dims):
    out = dot(parts[0], ones, dims)
    for part in parts[1:]:
        out = out + dot(part, ones, dims)
    return out


def mm_exact_left(ones, parts, dims):
    out = dot(ones, parts[0], dims)
    for part in parts[1:]:
        out = out + dot(ones, part, dims)
    return out


def iota(shape, dim):
    return lax.broadcasted_iota(jnp.int32, shape, dim)


def head_ones(heads, width):
    row, col = iota((heads, width), 0), iota((heads, width), 1)
    return jnp.where((col >= row * P_SIZE) & (col < (row + 1) * P_SIZE), 1.0, 0.0).astype(BF)


def spread(per_head, ones):
    return mm_exact(split3(per_head), ones, TN)


def head_sums(a, ones):
    return mm_exact_left(ones, split3(a), NT)


def columns(per_head, eye):
    return mm_exact_left(eye, split3(per_head), NT)


def to_row(column):
    heads = column.shape[0]
    same = iota((heads, heads), 0) == iota((heads, heads), 1)
    return jnp.sum(jnp.where(same, column, 0.0), axis=0, keepdims=True)


def scalars(ref, shape, dim, each):
    place = iota(shape, dim)
    out = jnp.full(shape, ref[0], F32)
    for i in range(1, ref.shape[0]):
        out = jnp.where(place >= i * each, ref[i], out)
    return out


def triangle(rows, upper):
    row, col = iota((rows, rows), 0), iota((rows, rows), 1)
    return jnp.where(col >= row if upper else row >= col, 1.0, 0.0).astype(BF)


def convolved(ext_ref, start, weight, bias, row_count):
    pre_act = bias
    for tap in range(weight.shape[0]):
        pre_act = pre_act + weight[tap : tap + 1] * ext_ref[start + tap : start + tap + row_count, :]
    return pre_act


def softplus(z):
    return jnp.maximum(z, 0.0) + jnp.log1p(jnp.exp(-jnp.abs(z)))


def sigmoid(z):
    return 1.0 / (1.0 + jnp.exp(-z))


def valid_rows(lengths_ref, seq, row_count, dim):
    first = lax.axis_index("inner") * row_count
    shape = (row_count, 1) if dim == 0 else (1, row_count)
    return jnp.where(first + iota(shape, dim) < lengths_ref[seq], 1.0, 0.0)


def remote(src, dst, send, recv, **where):
    return pltpu.make_async_remote_copy(
        src_ref=src, dst_ref=dst, send_sem=send, recv_sem=recv, device_id=where, device_id_type=MESH
    )


def greet(**where):
    pl.semaphore_signal(pltpu.get_barrier_semaphore(), inc=1, device_id=where, device_id_type=MESH)


def loop(first, count, do):
    def body(i, carry):
        do(i)
        return carry

    lax.fori_loop(first, count, body, 0)


INS = (
    "lengths_in", "sb_in", "dl_in", "skip_in", "x_in", "bc_in", "step_in", "og_in", "wx_in", "bx_in", "wbc_in", "bbc_in",
)
OUTS = (
    "mixed_out", "gx_out", "gbc_out", "dstep_out", "wx_out", "bx_out", "wbc_out", "bbc_out", "sb_out", "dl_out", "skip_out",
)
DIRECT = 4


def layout(seqs, row_count, wide, both, heads, taps, edge, groups, chips, near, pieces):
    state, rows = both // 2, seqs * row_count // groups
    blocks, flat = chips // near, (seqs * wide, state)
    smem, i32 = pltpu.SMEM, jnp.int32
    return {
        "lengths": smem((seqs,), i32), "sb": smem((heads,), F32), "dl": smem((heads,), F32), "skip": smem((heads,), F32),
        "x": VMEM((seqs, row_count, wide), BF), "bc": VMEM((seqs, row_count, both), BF),
        "step": VMEM((seqs, heads, row_count), F32), "og": VMEM((seqs, row_count, wide), BF),
        "wx": VMEM((taps, wide), F32), "bx": VMEM((1, wide), F32), "wbc": VMEM((taps, both), F32),
        "bbc": VMEM((1, both), F32), "load": DMA((len(INS),)),
        "px": VMEM((seqs, edge, wide), BF), "pbc": VMEM((seqs, edge, both), BF), "nbc": VMEM((seqs, edge, both), BF),
        "mixed": VMEM((seqs, row_count, wide), BF), "gx": VMEM((seqs, row_count, wide), BF),
        "gx_tail": VMEM((seqs, edge, wide), F32), "gbc": VMEM((seqs, row_count, both), BF),
        "dstep": VMEM((seqs, heads, row_count), F32), "store": DMA((DIRECT,)),
        "extx": VMEM((seqs, edge + row_count, wide), F32), "extbc": VMEM((seqs, 2 * edge + row_count, both), F32),
        "feat": VMEM((seqs, row_count, wide), F32), "slope": VMEM((seqs, row_count, wide), F32),
        "kq": VMEM((seqs, row_count, both), F32), "slope_bc": VMEM((seqs, row_count, both), F32),
        "weight": VMEM((seqs, row_count, wide), F32), "grown": VMEM((seqs, row_count, wide), F32),
        "dt": VMEM((seqs, heads, row_count), F32), "cum": VMEM((seqs, heads, row_count), F32),
        "within": VMEM((seqs, row_count, wide), F32), "dfeat": VMEM((seqs, row_count, wide), F32),
        "dscores": VMEM((seqs, row_count, row_count), F32),
        "row_part": VMEM((seqs, heads, row_count), F32), "col_part": VMEM((seqs, heads, row_count), F32),
        "dpre": VMEM((row_count + 8, wide), F32), "lead": VMEM((seqs, 8, wide), F32),
        "dkq": VMEM((seqs * row_count, both), F32), "total": VMEM((seqs * row_count, both), F32),
        "next_total": VMEM((seqs, 8, both), F32), "next_lead": VMEM((seqs, 8, wide), F32),
        "dpre_bc": VMEM((row_count + 8, both), F32), "pad": VMEM((edge + 8, wide), F32),
        "edge_send": DMA((4,)), "edge_recv": DMA((4,)),
        "own": VMEM((2,) + flat, F32), "other": VMEM(flat, F32), "io": VMEM((2,) + flat, F32), "after": VMEM(flat, F32),
        "decay": VMEM((seqs, heads, state), F32), "odecay": VMEM((seqs, heads, state), F32),
        "joined": VMEM(flat, F32), "both": VMEM((seqs, heads, state), F32),
        "later": VMEM(flat, F32), "later_in": VMEM(flat, F32), "shrink": VMEM((seqs, heads, state), F32),
        "shrink_in": VMEM((seqs, heads, state), F32), "ahead": VMEM(flat, F32), "beyond": VMEM(flat, F32),
        "swap_send": DMA((pieces,)), "swap_recv": DMA((pieces,)), "hand_send": DMA((pieces,)), "hand_recv": DMA((pieces,)),
        "later_send": DMA((pieces + 1,)), "later_recv": DMA((pieces + 1,)),
        "step_send": DMA((pieces,)), "skip_send": DMA((pieces,)), "chain_recv": DMA((pieces,)),
        "slots": VMEM((groups - 1, rows, both), F32),
        "scatter_send": DMA((groups,)), "scatter_recv": DMA((groups,)),
        "gather_send": DMA((groups,)), "gather_recv": DMA((groups,)),
        "rim_send": DMA((groups,)), "rim_recv": DMA((seqs + 1,)), "lead_send": DMA((1,)),
        "outer": VMEM((groups, 16, state), F32), "outer_send": DMA((groups,)), "outer_recv": DMA((groups,)),
        "x_mine": VMEM((8, wide), F32), "x_mate": VMEM((8, wide), F32), "x_near": VMEM((near, 8, wide), F32),
        "x_far": VMEM((blocks, 8, wide), F32), "x_send": DMA((near + blocks,)), "x_recv": DMA((near + blocks,)),
        "p_mine": VMEM((16, state), F32), "p_mate": VMEM((16, state), F32), "p_near": VMEM((near, 16, state), F32),
        "p_far": VMEM((blocks, 16, state), F32), "p_send": DMA((near + blocks,)), "p_recv": DMA((near + blocks,)),
    }


def activate(r, seq, first, rows):
    edge, taps = r.px.shape[1], r.wx.shape[0]
    where = pl.ds(first, rows)
    for ext, weight, bias, value, slope in (
        (r.extx, r.wx, r.bx, r.feat, r.slope),
        (r.extbc, r.wbc, r.bbc, r.kq, r.slope_bc),
    ):
        pre = convolved(ext.at[seq], edge - (taps - 1) + first, weight[...], bias[...], rows)
        gate = sigmoid(pre)
        value[seq, where, :] = pre * gate
        slope[seq, where, :] = gate * (1.0 + pre * (1.0 - gate))


def local_states(r, seq):
    state = r.kq.shape[2] // 2
    dy = r.og[seq].astype(F32)
    keys, queries = split(r.kq[seq, :, :state]), split(r.kq[seq, :, state:])
    return (
        mm(split(r.weight[seq] * r.feat[seq]), keys, TN),
        mm(split(r.grown[seq] * dy), queries, TN),
    )


def inside(r, seq):
    row_count, wide = r.feat.shape[1:]
    heads, state = r.dt.shape[1], r.kq.shape[2] // 2
    dy = r.og[seq].astype(F32) * valid_rows(r.lengths, seq, row_count, 0)
    dy_b = dy.astype(BF)
    feats, keys, queries = split(r.feat[seq]), split(r.kq[seq, :, :state]), split(r.kq[seq, :, state:])
    lane = iota((1, wide), 1)
    row, col = iota((row_count, row_count), 0), iota((row_count, row_count), 1)
    causal = row >= col
    eye = jnp.where(row == col, 1.0, 0.0).astype(BF)
    dt, cum = r.dt[seq], r.cum[seq]
    cum_cols = columns(cum, eye)
    scores = mm(queries, keys, NT)
    within = jnp.zeros((row_count, wide), F32)
    dfeat = jnp.zeros((row_count, wide), F32)
    dscores = jnp.zeros((row_count, row_count), F32)
    row_sums, col_sums = [], []
    for head in range(heads):
        gap = cum_cols[:, head : head + 1] - cum[head : head + 1, :]
        decays = jnp.where(causal, jnp.exp(jnp.where(causal, gap, 0.0)), 0.0)
        stepped = decays * dt[head : head + 1, :]
        mixing = stepped * scores
        here = (lane >= head * P_SIZE) & (lane < (head + 1) * P_SIZE)
        within = jnp.where(here, mm(split(mixing), feats, NN), within)
        dfeat = jnp.where(here, mm(split(mixing.T), (dy_b,), NN), dfeat)
        dmixing = mm((jnp.where(here, dy, 0.0).astype(BF),), feats, NT)
        dscores = dscores + dmixing * stepped
        row_sums.append(jnp.sum(dmixing * mixing, axis=1, keepdims=True))
        col_sums.append(jnp.sum(dmixing * decays * scores, axis=0, keepdims=True))
    r.within[seq] = within
    r.dfeat[seq] = dfeat
    r.dscores[seq] = dscores
    r.row_part[seq] = mm_exact(split3(jnp.concatenate(row_sums, axis=1)), eye, TN)
    r.col_part[seq] = jnp.concatenate(col_sums, axis=0)


def rows_back(r, seq):
    row_count, wide = r.feat.shape[1:]
    state = r.kq.shape[2] // 2
    block, rows = pl.ds(seq * wide, wide), pl.ds(seq * row_count, row_count)
    dy = r.og[seq].astype(F32) * valid_rows(r.lengths, seq, row_count, 0)
    keys, queries = split(r.kq[seq, :, :state]), split(r.kq[seq, :, state:])
    dscores = r.dscores[seq]
    r.dkq[rows, state:] = mm(split(dscores), keys, NN) + mm(split(r.grown[seq] * dy), split(r.io[0, block, :]), NN)
    r.dkq[rows, :state] = mm(split(dscores.T), queries, NN) + mm(
        split(r.weight[seq] * r.feat[seq]), split(r.io[1, block, :]), NN
    )


def heads_back(r, seq):
    row_count, wide = r.feat.shape[1:]
    edge, taps, heads, state = r.px.shape[1], r.wx.shape[0], r.dt.shape[1], r.kq.shape[2] // 2
    block = pl.ds(seq * wide, wide)
    valid = valid_rows(r.lengths, seq, row_count, 0)
    dy = r.og[seq].astype(F32) * valid
    feat, dt, cum = r.feat[seq], r.dt[seq], r.cum[seq]
    incoming, later = r.io[0, block, :], r.io[1, block, :]
    ones = head_ones(heads, wide)
    skip = scalars(r.skip, (1, wide), 1, P_SIZE)
    carried = mm(split(r.kq[seq, :, state:]), split(incoming), NT) * r.grown[seq]
    r.mixed[seq] = ((r.within[seq] + carried + skip * feat) * valid).astype(BF)
    back = mm(split(r.kq[seq, :, :state]), split(later), NT)
    dfeat = r.dfeat[seq] + skip * dy + r.weight[seq] * back

    total = cum[:, row_count - 1 :]
    col_part = r.col_part[seq]
    back_left = head_sums(feat * back, ones) * jnp.exp(total - cum)
    dcum = r.row_part[seq] + head_sums(dy * carried, ones) - (col_part + back_left) * dt
    later_in = jnp.sum(mm_exact_left(ones, split3(later * incoming), NN), axis=1, keepdims=True)
    dtotal = jnp.sum(back_left * dt, axis=1, keepdims=True) + later_in * jnp.exp(total)
    drun = mm_exact(split3(dcum), triangle(row_count, False), NN) + dtotal
    rate = -jnp.exp(scalars(r.dl, (heads, 1), 0, 1))
    z = r.step[seq] + scalars(r.sb, (heads, 1), 0, 1)
    dstep = (col_part + back_left + drun * rate) * valid_rows(r.lengths, seq, row_count, 1) * sigmoid(z)
    r.dstep[seq] = dstep
    ddecay = jnp.sum(drun * dt, axis=1, keepdims=True) * rate
    dskip = jnp.sum(head_sums(dy * feat, ones), axis=1, keepdims=True)

    dpre = dfeat * r.slope[seq]
    r.lead[seq] = dpre[:8, :]
    r.dpre[:row_count, :] = dpre
    r.dpre[row_count:, :] = jnp.zeros((8, wide), F32)
    gx = jnp.zeros((row_count, wide), F32)
    for tap in range(taps):
        shift = taps - 1 - tap
        gx = gx + r.wx[tap : tap + 1, :] * r.dpre[shift : shift + row_count, :]
    r.gx[seq] = gx.astype(BF)
    r.gx_tail[seq] = gx[row_count - edge :, :]
    start = edge - (taps - 1)
    for tap in range(taps):
        term = dpre * r.extx[seq, start + tap : start + tap + row_count, :]
        r.x_mine[tap : tap + 1, :] += jnp.sum(term, axis=0, keepdims=True)
    r.x_mine[taps : taps + 1, :] += jnp.sum(dpre, axis=0, keepdims=True)
    for i, part in enumerate((jnp.sum(dstep, axis=1, keepdims=True), ddecay, dskip)):
        r.x_mine[taps + 1 + i : taps + 2 + i, :heads] += to_row(part)


def last_rows(r, seq, has_after):
    edge, taps, row_count = r.px.shape[1], r.wx.shape[0], r.x.shape[1]
    lead, wide = r.next_lead.shape[1:]
    r.pad[:edge, :] = jnp.zeros((edge, wide), F32)
    r.pad[edge:, :] = r.next_lead[seq] * has_after
    tail = r.gx_tail[seq]
    for tap in range(taps):
        shift = taps - 1 - tap
        tail = tail + r.wx[tap : tap + 1, :] * r.pad[shift : shift + edge, :]
    r.gx[seq, row_count - edge :, :] = tail.astype(BF)


def bc_grads(r, seq, has_after):
    edge, taps, row_count = r.px.shape[1], r.wx.shape[0], r.x.shape[1]
    lead, both = r.next_total.shape[1:]
    pre = convolved(r.extbc.at[seq], edge - (taps - 1) + row_count, r.wbc[...], r.bbc[...], lead)
    gate = sigmoid(pre)
    slope = gate * (1.0 + pre * (1.0 - gate))
    r.dpre_bc[:row_count, :] = r.total[seq * row_count : (seq + 1) * row_count, :] * r.slope_bc[seq]
    r.dpre_bc[row_count:, :] = r.next_total[seq] * slope * has_after
    grad = jnp.zeros((row_count, both), F32)
    for tap in range(taps):
        shift = taps - 1 - tap
        grad = grad + r.wbc[tap : tap + 1, :] * r.dpre_bc[shift : shift + row_count, :]
    r.gbc[seq] = grad.astype(BF)


def far_place(chips, core, place):
    return jnp.where(core == 0, place, chips - 1 - place) * 2 + core


def mixer_kernel(names, groups, size, near, pieces, *refs):
    r = types.SimpleNamespace(**dict(zip(names, refs)))
    seqs, row_count, wide = r.x.shape
    both, heads, edge, taps = r.bc.shape[2], r.dt.shape[1], r.px.shape[1], r.wx.shape[0]
    state, chips = both // 2, size // 2
    blocks = chips // near
    me, inner = lax.axis_index("outer"), lax.axis_index("inner")
    after, before = lax.rem(inner + 1, size), lax.rem(inner + size - 1, size)
    chip, core = inner // 2, lax.rem(inner, 2)
    mate = chip * 2 + 1 - core
    chip_block, chip_spot = chip // near, lax.rem(chip, near)
    shares = groups // seqs
    owner = lax.rem(me, shares) == 0

    def near_peer(d):
        return (chip_block * near + lax.rem(chip_spot + d, near)) * 2 + core

    def far_peer(d):
        return (lax.rem(chip_block + d, blocks) * near + chip_spot) * 2 + core

    def around(d):
        return lax.rem(me + d, groups)

    ahead = lax.rem(chip + 1 - 2 * core + chips, chips) * 2 + core
    behind = lax.rem(chip - 1 + 2 * core + chips, chips) * 2 + core
    loads = {
        name: pltpu.make_async_copy(getattr(r, name), getattr(r, name[:-3]), r.load.at[i]) for i, name in enumerate(INS)
    }
    for copy in loads.values():
        copy.start()
    peers = [after, before, mate, ahead, behind]
    peers += [near_peer(d) for d in range(1, near)] + [far_peer(d) for d in range(1, blocks)]
    for other in peers:
        greet(inner=other)
    loop(1, groups, lambda d: greet(outer=around(d)))
    for seq in range(seqs):
        greet(outer=seq * shares, inner=after)
    for name in ("lengths_in", "sb_in", "dl_in", "step_in"):
        loads[name].wait()

    ones = head_ones(heads, wide)
    rate = -jnp.exp(scalars(r.dl, (heads, 1), 0, 1))
    bias = scalars(r.sb, (heads, 1), 0, 1)
    for seq in range(seqs):
        dt = softplus(r.step[seq] + bias) * valid_rows(r.lengths, seq, row_count, 1)
        cum = mm_exact(split3(dt * rate), triangle(row_count, True), NN)
        r.dt[seq] = dt
        r.cum[seq] = cum
        r.decay[seq] = jnp.broadcast_to(jnp.exp(cum[:, row_count - 1 :]), (heads, state))
    r.x_mine[...] = jnp.zeros(r.x_mine.shape, F32)
    r.p_mine[...] = jnp.zeros(r.p_mine.shape, F32)
    for name in INS:
        if name not in ("lengths_in", "sb_in", "dl_in", "step_in"):
            loads[name].wait()

    def begin(seq):
        dt, cum = r.dt[seq], r.cum[seq]
        r.weight[seq] = spread(jnp.exp(cum[:, row_count - 1 :] - cum) * dt, ones)
        r.grown[seq] = spread(jnp.exp(cum), ones) * valid_rows(r.lengths, seq, row_count, 0)
        r.extx[seq, edge:, :] = r.x[seq].astype(F32)
        r.extbc[seq, edge : edge + row_count, :] = r.bc[seq].astype(F32)
        activate(r, seq, edge, row_count - edge)

    pl.semaphore_wait(
        pltpu.get_barrier_semaphore(), len(peers) + groups - 1 + jnp.where(owner, groups, 0)
    )

    tail = pl.ds(row_count - edge, edge)
    rims = [
        remote(r.bc.at[:, tail, :], r.pbc, r.edge_send.at[1], r.edge_recv.at[1], inner=after),
        remote(r.x.at[:, tail, :], r.px, r.edge_send.at[0], r.edge_recv.at[0], inner=after),
        remote(r.bc.at[:, pl.ds(0, edge), :], r.nbc, r.edge_send.at[2], r.edge_recv.at[2], inner=before),
    ]
    for copy in rims:
        copy.start()
    decays = remote(r.decay, r.odecay, r.edge_send.at[3], r.edge_recv.at[3], inner=mate)
    decays.start()
    for seq in range(seqs):
        begin(seq)

    rows = seqs * wide // pieces
    per_head, per_seq = P_SIZE // rows, wide // rows

    def piece(j):
        return pl.ds(pl.multiple_of(j * rows, rows), rows)

    def swap(j):
        return remote(
            r.own.at[1 - core, piece(j), :], r.other.at[piece(j), :], r.swap_send.at[j], r.swap_recv.at[j], inner=mate
        )

    keep = jnp.where(inner > 0, 1.0, 0.0)
    rims[0].wait_recv()
    rims[1].wait_recv()
    for seq in range(seqs):
        r.extx[seq, :edge, :] = r.px[seq].astype(F32) * keep
        r.extbc[seq, :edge, :] = r.pbc[seq].astype(F32) * keep
        activate(r, seq, 0, edge)
        for kind, value in enumerate(local_states(r, seq)):
            r.own[kind, seq * wide : (seq + 1) * wide, :] = value
        loop(seq * per_seq, (seq + 1) * per_seq, lambda j: swap(j).start())

    place = jnp.where(core == 0, chip, chips - 1 - chip)
    block = jnp.maximum(place - 1, 0) // near
    spot = place - 1 - block * near
    opens, ends = place == 0, spot == near - 1
    summed = (block > 0) & (block < blocks - 1)
    skips = summed & (spot == 0)
    steps = (place < chips - 1) & jnp.logical_not(summed & ends)
    busy_first = (block < blocks - 2) | ((block == blocks - 2) & (spot == 0))
    further = far_place(chips, core, place + near)

    def seq_head(j):
        head = j // per_head
        return head // heads, pl.ds(lax.rem(head, heads), 1)

    def send_later(j):
        return remote(
            r.later.at[piece(j), :], r.later_in.at[piece(j), :], r.later_send.at[j], r.later_recv.at[j], inner=behind
        )

    def send_shrink():
        return remote(r.shrink, r.shrink_in, r.later_send.at[pieces], r.later_recv.at[pieces], inner=behind)

    def step(j):
        return remote(
            r.ahead.at[piece(j), :], r.io.at[core, piece(j), :], r.step_send.at[j], r.chain_recv.at[j], inner=ahead
        )

    def skip(j):
        return remote(
            r.beyond.at[piece(j), :], r.io.at[core, piece(j), :], r.skip_send.at[j], r.chain_recv.at[j], inner=further
        )

    def hand(j, kind):
        return remote(
            r.after.at[piece(j), :], r.io.at[kind, piece(j), :], r.hand_send.at[j], r.hand_recv.at[j], inner=mate
        )

    decays.wait_recv()
    r.both[...] = r.decay[...] * r.odecay[...]

    @pl.when(summed & ends)
    def _():
        r.shrink[...] = r.both[...]
        send_shrink().start()

    @pl.when(opens)
    def _():
        r.io[core] = jnp.zeros((seqs * wide, state), F32)

    def join(j):
        swap(j).wait_recv()
        seq, head = seq_head(j)
        joined = r.odecay[seq, head, :] * r.own[core, piece(j), :] + r.other[piece(j), :]
        r.joined[piece(j), :] = joined

        @pl.when(summed & ends)
        def _():
            r.later[piece(j), :] = joined
            send_later(j).start()

        @pl.when(opens)
        def _():
            r.ahead[piece(j), :] = joined
            step(j).start()

    loop(0, pieces, join)

    @pl.when(summed & jnp.logical_not(ends))
    def _():
        send_shrink().wait_recv()
        r.shrink[...] = r.both[...] * r.shrink_in[...]

        @pl.when(spot > 0)
        def _():
            send_shrink().start()

        def sum_up(j):
            seq, head = seq_head(j)
            send_later(j).wait_recv()
            r.later[piece(j), :] = r.shrink_in[seq, head, :] * r.joined[piece(j), :] + r.later_in[piece(j), :]

            @pl.when(spot > 0)
            def _():
                send_later(j).start()

        loop(0, pieces, sum_up)

    @pl.when(jnp.logical_not(busy_first))
    def _():
        loop(0, seqs, lambda seq: inside(r, seq))

    def go_on(j):
        seq, head = seq_head(j)
        r.ahead[piece(j), :] = r.both[seq, head, :] * r.io[core, piece(j), :] + r.joined[piece(j), :]
        step(j).start()

    def pass_on(j):
        seq, head = seq_head(j)

        @pl.when(jnp.logical_not(opens))
        def _():
            step(j).wait_recv()

        @pl.when(skips)
        def _():
            r.beyond[piece(j), :] = r.shrink[seq, head, :] * r.io[core, piece(j), :] + r.later[piece(j), :]
            skip(j).start()

        @pl.when(steps & jnp.logical_not(skips | opens))
        def _():
            go_on(j)

        r.after[piece(j), :] = r.decay[seq, head, :] * r.io[core, piece(j), :] + r.own[core, piece(j), :]
        hand(j, core).start()

    loop(0, pieces, pass_on)

    @pl.when(skips)
    def _():
        loop(0, pieces, go_on)

    @pl.when(busy_first)
    def _():
        loop(0, seqs, lambda seq: inside(r, seq))

    loop(0, pieces, lambda j: hand(j, 1 - core).wait_recv())

    share_rows = seqs * row_count // groups

    def share_of(index):
        return pl.ds(pl.multiple_of(index * share_rows, share_rows), share_rows)

    def scatter(d):
        to = around(d)
        return remote(
            r.dkq.at[share_of(to), :], r.slots.at[d - 1], r.scatter_send.at[d], r.scatter_recv.at[d], outer=to
        )

    def gather(d, source):
        part = r.total.at[share_of(source), :]
        return remote(part, part, r.gather_send.at[d], r.gather_recv.at[d], outer=around(d))

    def gather_params(d, source):
        part = r.outer.at[source]
        return remote(part, part, r.outer_send.at[d], r.outer_recv.at[d], outer=around(d))

    lead = r.next_total.shape[1]

    def rim(to, seq):
        return remote(
            r.total.at[pl.ds(seq * row_count, lead), :], r.next_total.at[seq], r.rim_send.at[to], r.rim_recv.at[seq],
            outer=to, inner=before,
        )

    def source(d):
        return lax.rem(me + groups - d, groups)

    leaves = []

    def stage(buf, index, many, peer, send, recv, first):
        for d in range(1, many):
            remote(buf.at[index], buf.at[index], send.at[first + d], recv.at[first + d], inner=peer(d)).start()

        def finish():
            for d in range(1, many):
                part = buf.at[lax.rem(index + many - d, many)]
                remote(part, part, send.at[first + d], recv.at[first + d], inner=peer(d)).wait_recv()
            total = buf[0]
            for k in range(1, many):
                total = total + buf[k]
            return total

        def leave():
            for d in range(1, many):
                part = buf.at[index]
                remote(part, part, send.at[first + d], recv.at[first + d], inner=peer(d)).wait_send()

        leaves.append(leave)
        return finish

    for seq in range(seqs):
        rows_back(r, seq)

    loop(1, groups, lambda d: scatter(d).start())

    start = edge - (taps - 1)
    for seq in range(seqs):
        dpre = r.dkq[seq * row_count : (seq + 1) * row_count, :] * r.slope_bc[seq]
        for tap in range(taps + 1):
            term = dpre if tap == taps else dpre * r.extbc[seq, start + tap : start + tap + row_count, :]
            term = jnp.sum(term, axis=0, keepdims=True)
            r.p_mine[tap : tap + 1, :] += term[:, :state]
            r.p_mine[8 + tap : 9 + tap, :] += term[:, state:]
    p_mate = remote(r.p_mine, r.p_mate, r.p_send.at[0], r.p_recv.at[0], inner=mate)
    p_mate.start()
    p_mate.wait()
    r.p_near[chip_spot] = r.p_mine[...] + r.p_mate[...]
    p_finish = stage(r.p_near, chip_spot, near, near_peer, r.p_send, r.p_recv, 0)
    for seq in range(seqs):
        heads_back(r, seq)
    x_mate = remote(r.x_mine, r.x_mate, r.x_send.at[0], r.x_recv.at[0], inner=mate)
    x_mate.start()
    leads = remote(r.lead, r.next_lead, r.lead_send.at[0], r.rim_recv.at[seqs], inner=before)
    leads.start()
    stores = [
        pltpu.make_async_copy(getattr(r, name[:-4]), getattr(r, name), r.store.at[i])
        for i, name in enumerate(OUTS[:DIRECT])
    ]
    stores[0].start()
    stores[3].start()
    r.p_far[chip_block] = p_finish()
    p_finish = stage(r.p_far, chip_block, blocks, far_peer, r.p_send, r.p_recv, near)
    x_mate.wait()
    r.x_near[chip_spot] = r.x_mine[...] + r.x_mate[...]
    x_finish = stage(r.x_near, chip_spot, near, near_peer, r.x_send, r.x_recv, 0)

    loop(1, groups, lambda d: scatter(d).wait_recv())
    acc = r.dkq[share_of(me), :]
    for d in range(groups - 1):
        acc = acc + r.slots[d]
    r.total[share_of(me), :] = acc
    loop(1, groups, lambda d: gather(d, me).start())

    @pl.when(owner)
    def _():
        loop(0, groups, lambda to: rim(to, me // shares).start())

    r.x_far[chip_block] = x_finish()
    x_finish = stage(r.x_far, chip_block, blocks, far_peer, r.x_send, r.x_recv, near)
    for copy in rims:
        copy.wait_send()
    decays.wait_send()
    leads.wait_send()

    def sent(j):
        swap(j).wait_send()
        hand(j, core).wait_send()

        @pl.when(summed & (spot > 0))
        def _():
            send_later(j).wait_send()

        @pl.when(steps)
        def _():
            step(j).wait_send()

        @pl.when(skips)
        def _():
            skip(j).wait_send()

    loop(0, pieces, sent)

    @pl.when(summed & (spot > 0))
    def _():
        send_shrink().wait_send()

    loop(1, groups, lambda d: scatter(d).wait_send())
    r.outer[me] = p_finish()
    loop(1, groups, lambda d: gather_params(d, me).start())
    loop(1, groups, lambda d: gather(d, source(d)).wait_recv())
    for seq in range(seqs):
        rim(me, seq).wait_recv()
    has_after = jnp.where(inner < size - 1, 1.0, 0.0)
    rims[2].wait_recv()
    leads.wait_recv()
    for seq in range(seqs):
        r.extbc[seq, edge + row_count :, :] = r.nbc[seq].astype(F32)
        last_rows(r, seq, has_after)
        bc_grads(r, seq, has_after)
    stores[1].start()
    stores[2].start()
    total = x_finish()
    r.wx_out[...] = total[:taps]
    r.bx_out[...] = total[taps : taps + 1]
    for i, out in enumerate((r.sb_out, r.dl_out, r.skip_out)):
        out[...] = total[taps + 1 + i : taps + 2 + i, :heads]

    for leave in leaves:
        leave()
    @pl.when(owner)
    def _():
        loop(0, groups, lambda to: rim(to, me // shares).wait_send())

    def gone(d):
        gather(d, me).wait_send()

    loop(1, groups, gone)
    for copy in stores:
        copy.wait()
    loop(1, groups, lambda d: gather_params(d, source(d)).wait_recv())
    total = r.outer[0]
    for k in range(1, groups):
        total = total + r.outer[k]
    r.wbc_out[:, :state] = total[:taps]
    r.wbc_out[:, state:] = total[8 : 8 + taps]
    r.bbc_out[:, :state] = total[taps : taps + 1]
    r.bbc_out[:, state:] = total[8 + taps : 9 + taps]

    def drain(d):
        gather_params(d, me).wait_send()

    loop(1, groups, drain)


def mixer(lengths, sb, dl, skip, x_raw, bc_raw, step, output_grad, wx, bx, wbc, bbc, groups, size, edge):
    seqs, row_count, wide = x_raw.shape
    both, heads, taps = bc_raw.shape[2], step.shape[1], wx.shape[0]
    state, chips = both // 2, size // 2
    near = 4 if chips % 4 == 0 else 1
    pieces = 16
    scratch = layout(seqs, row_count, wide, both, heads, taps, edge, groups, chips, near, pieces)
    shapes = (
        ((seqs, row_count, wide), BF), ((seqs, row_count, wide), BF), ((seqs, row_count, both), BF),
        ((seqs, heads, row_count), F32), ((taps, wide), F32), ((1, wide), F32), ((taps, both), F32), ((1, both), F32),
        ((1, heads), F32), ((1, heads), F32), ((1, heads), F32),
    )
    return pl.pallas_call(
        functools.partial(mixer_kernel, INS + OUTS + tuple(scratch), groups, size, near, pieces),
        name="mixer",
        out_shape=[jax.ShapeDtypeStruct(*s) for s in shapes],
        in_specs=[pl.BlockSpec(memory_space=pltpu.HBM)] * len(INS),
        out_specs=[pl.BlockSpec(memory_space=pltpu.HBM)] * DIRECT + [pl.BlockSpec(memory_space=VMEM)] * (len(OUTS) - DIRECT),
        scratch_shapes=list(scratch.values()),
        compiler_params=pltpu.CompilerParams(collective_id=0, has_side_effects=True, vmem_limit_bytes=LIMIT),
    )(lengths, sb, dl, skip, x_raw, bc_raw, step, output_grad, wx, bx, wbc, bbc)


def hand_on_kernel(*refs):
    count = len(OUTS)
    for taken, given in zip(refs[:count], refs[count:]):
        given[...] = taken[...]


def hand_on(arrays):
    specs = [pl.BlockSpec(memory_space=VMEM)] * len(arrays)
    return pl.pallas_call(
        hand_on_kernel,
        name="hand_on",
        out_shape=[jax.ShapeDtypeStruct(a.shape, a.dtype) for a in arrays],
        in_specs=specs,
        out_specs=specs,
        compiler_params=pltpu.CompilerParams(vmem_limit_bytes=LIMIT),
    )(*arrays)


def per_device(
    sizes, x_raw, bc_raw, step_raw, lengths, conv_weight_x, conv_bias_x, conv_weight_bc, conv_bias_bc, step_bias,
    decay_log, skip_gain, output_grad,
):
    groups, size = sizes
    edge = 16
    bx, bbc = conv_bias_x[None], conv_bias_bc[None]
    step = jnp.swapaxes(step_raw, 1, 2)
    mixed, gx, gbc, dstep, wx, bx_g, wbc, bbc_g, sb_g, dl_g, skip_g = hand_on(
        mixer(
            lengths, step_bias, decay_log, skip_gain, x_raw, bc_raw, step, output_grad, conv_weight_x, bx, conv_weight_bc,
            bbc, groups, size, edge,
        )
    )
    return (mixed, gx, gbc, jnp.swapaxes(dstep, 1, 2), wx, bx_g[0], wbc, bbc_g[0], sb_g[0], dl_g[0], skip_g[0])


def solution(mesh):
    rows_and_heads = P(None, "inner", "outer")
    return jax.shard_map(
        functools.partial(per_device, (mesh.shape["outer"], mesh.shape["inner"])),
        mesh=mesh,
        in_specs=(
            rows_and_heads, P(None, "inner", None), rows_and_heads, P(), P(None, "outer"), P("outer"), P(), P(),
            P("outer"), P("outer"), P("outer"), rows_and_heads,
        ),
        out_specs=(
            rows_and_heads, rows_and_heads, P(None, "inner", None), rows_and_heads, P(None, "outer"), P("outer"), P(),
            P(), P("outer"), P("outer"), P("outer"),
        ),
        check_vma=False,
    )
```
